256 devices in a mesh: grp: 2 (over x_hi), pb: 8 (over y, core), ha: 16 (over x_lo, z).
Axes of the slice: x: 4 (x_hi: 2, x_lo: 2; x = x_hi * 2 + x_lo), y: 4, z: 8, core: 2. Of those that a mesh axis runs over, the one named last changes fastest.
Arguments:
- hyena_proj: bfloat16 [3, 4096, 4096], P(None, 'ha', ('grp', 'pb')), may hold values from -6 to 6
- dskip: float32 [4096], P(('grp', 'pb')), may hold values from -1 to 1
- filters: float32 [3, 2, 4096, 4096], P(None, None, ('grp', 'pb', 'ha')), may hold values from -6 to 6
- resident: float32 [2, 2, 4096, 4096], P(None, None, ('grp', 'pb', 'ha')), may hold values from -384 to 384
- cache_kv: bfloat16 [2, 4096, 4096], P(None, 'ha', ('grp', 'pb'))
- norm_gain: float32 [4096], replicated, may hold values from 0.5 to 1.5
- w_qkv: bfloat16 [4096, 3, 4096], P(None, None, ('grp', 'pb'))
- w_out: bfloat16 [4096, 4096], P(None, ('grp', 'pb')), may hold values from -0.09375 to 0.09375
Outputs:
- mixed: bfloat16 [4096, 4096], P('ha', ('grp', 'pb'))
- block_spectrum: float32 [2, 4096, 4096], P(None, ('grp', 'pb', 'ha'))
The draws below stay inside these ranges and needn't reach their ends.
All inputs are finite; a program needn't handle non-finite values.
Results may differ from the reference program's by a relative error of at most 0.015.
Values may be sent and summed in bfloat16 or wider, within the bound.
No kernel may reach another device: no remote copies, remote signals or barrier semaphores. Data moves between devices by JAX's collectives and lax.ppermute only.
A program may use at most 128 MiB of HBM per device.

```python
import jax
import jax.numpy as jnp
from jax import lax

D = 4096
HEADS = 32
HEAD = 128
BLOCK = 4096
CACHE = 4096


def head_scales(key, low, high):
    picked = jax.random.uniform(jax.random.fold_in(key, 23), (HEADS,), jnp.float32)
    return jnp.repeat(low * (high / low) ** picked, HEAD)


def draw_cache_kv(key, part):
    column = head_scales(key, 2.0, 8.0)
    key = jax.random.fold_in(key, 7)
    base = jax.random.normal(key, (2, CACHE, D), jnp.float32)
    scales = jnp.stack([column, jnp.ones_like(column)])[:, None, :]
    return (base * scales).astype(jnp.bfloat16)


def draw_w_qkv(key, part):
    column = head_scales(key, 2.0, 8.0)
    key = jax.random.fold_in(key, 5)
    base = jax.random.normal(key, (D, 3, D), jnp.float32) * float(D) ** (-0.5)
    slots = jnp.stack([jnp.ones_like(column), column, jnp.ones_like(column)])[None, :, :]
    return (base * slots).astype(jnp.bfloat16)


def block_scale(stream_key, dims, shards, smallest, top_value):
    def one(position, shards_of):
        draws = jax.random.uniform(jax.random.fold_in(jax.random.fold_in(stream_key, 6), position), (shards_of,), jnp.float32, smallest / len(shards), top_value / len(shards))
        return jnp.repeat(jnp.exp(draws), dims[position] // shards_of).reshape((-1,) + (1,) * (len(dims) - position - 1))

    level = one(*shards[0])
    for cut in shards[1:]:
        level = level * one(*cut)
    return level


def gaussian(rng, dims, spread, bound, pieces=(), kind=jnp.bfloat16):
    entries = jax.random.normal(rng, dims, jnp.float32) * spread
    if len(pieces) > 0:
        entries = block_scale(rng, dims, pieces, -0.22, 0.18) * entries
    return jnp.clip(entries, min=-bound, max=bound).astype(kind)


def setup_inputs(seed: int = 0) -> dict:
    key_list = jax.random.split(jax.random.key(seed), 9)
    return {
        "hyena_proj": gaussian(key_list[0], (3, BLOCK, D), 1.0, 6.0, ((1, 16), (2, 16))),
        "dskip": jnp.clip(jax.random.uniform(key_list[1], (D,), jnp.float32, -1.0, 1.0) * block_scale(key_list[1], (D,), ((0, 16),), -0.4, 0.0), -1.0, 1.0),
        "filters": gaussian(key_list[2], (3, 2, D, BLOCK), 1.0, 6.0, ((2, 256),), jnp.float32),
        "resident": gaussian(key_list[3], (2, 2, D, BLOCK), 64.0, 384.0, ((2, 256),), jnp.float32),
        "cache_kv": draw_cache_kv(jax.random.fold_in(key_list[8], 71), 0),
        "norm_gain": jnp.clip(1.0 + 0.1 * jax.random.normal(key_list[5], (D,), jnp.float32), 0.5, 1.5),
        "w_qkv": draw_w_qkv(jax.random.fold_in(key_list[8], 71), 0),
        "w_out": gaussian(key_list[7], (D, D), D ** -0.5, 0.09375, ((1, 16),)),
    }


def rotate(values, positions):
    half = values.shape[-1] // 2
    freqs = 10000.0 ** (-jnp.arange(half, dtype=jnp.float32) / half)
    angles = positions.astype(jnp.float32)[:, None] * freqs[None, :]
    cosine = jnp.cos(angles)[:, None, :]
    sine = jnp.sin(angles)[:, None, :]
    first = values[..., :half]
    second = values[..., half:]
    return jnp.concatenate([first * cosine - second * sine, first * sine + second * cosine], axis=-1)

def one_head(inputs):
    queries, keys_now, values_now, keys_old, values_old = inputs
    all_keys = jnp.concatenate([keys_old, keys_now], axis=0).astype(jnp.float32)
    all_values = jnp.concatenate([values_old, values_now], axis=0).astype(jnp.float32)
    scores = jnp.dot(queries.astype(jnp.float32), all_keys.T) / jnp.sqrt(jnp.float32(HEAD))
    rows = jnp.arange(BLOCK, dtype=jnp.int32)[:, None]
    cols = jnp.arange(CACHE + BLOCK, dtype=jnp.int32)[None, :]
    allowed = cols <= rows + CACHE
    scores = jnp.where(allowed, scores, jnp.float32(-1e+30))
    top = lax.optimization_barrier(jnp.max(scores, axis=1, keepdims=True))
    expd = jnp.where(allowed, jnp.exp(scores - top), jnp.float32(0.0))
    total = lax.optimization_barrier(jnp.sum(expd, axis=1, keepdims=True))
    weights = expd.astype(jnp.bfloat16).astype(jnp.float32)
    return (jnp.dot(weights, all_values) / total).astype(jnp.bfloat16)

def reference(hyena_proj, dskip, filters, resident, cache_kv, norm_gain, w_qkv, w_out):
    gated = (hyena_proj[1].astype(jnp.float32) * hyena_proj[2].astype(jnp.float32)).astype(jnp.bfloat16)
    signal = gated.astype(jnp.float32)
    spectrum = jnp.fft.rfft(signal.T, n=2 * BLOCK, axis=1)[:, :BLOCK]
    real_part = jnp.real(spectrum).astype(jnp.float32)
    imag_part = jnp.imag(spectrum).astype(jnp.float32)
    sum_real = real_part * filters[0, 0] - imag_part * filters[0, 1]
    sum_imag = real_part * filters[0, 1] + imag_part * filters[0, 0]
    for which in (1, 2):
        old_real = resident[which - 1, 0]
        old_imag = resident[which - 1, 1]
        sum_real = sum_real + old_real * filters[which, 0] - old_imag * filters[which, 1]
        sum_imag = sum_imag + old_real * filters[which, 1] + old_imag * filters[which, 0]
    padding = jnp.zeros((D, 1), jnp.float32)
    padded_real = jnp.concatenate([sum_real, padding], axis=1)
    padded_imag = jnp.concatenate([sum_imag, padding], axis=1)
    conv = jnp.fft.irfft(lax.complex(padded_real, padded_imag), n=2 * BLOCK, axis=1)[:, :BLOCK]
    conv = conv.T.astype(jnp.bfloat16)
    hyena_out = (hyena_proj[0].astype(jnp.float32) * (conv.astype(jnp.float32) + dskip * signal)).astype(jnp.bfloat16)
    wide = hyena_out.astype(jnp.float32)
    meansq = lax.optimization_barrier(jnp.mean(wide * wide, axis=1, keepdims=True))
    normed = (wide * lax.rsqrt(meansq + 1e-05) * norm_gain).astype(jnp.bfloat16)
    qkv = jnp.dot(normed, w_qkv.reshape(D, 3 * D), preferred_element_type=jnp.float32)
    qkv = qkv.reshape(BLOCK, 3, HEADS, HEAD)
    positions = CACHE + jnp.arange(BLOCK, dtype=jnp.int32)
    queries = rotate(qkv[:, 0], positions).astype(jnp.bfloat16)
    keys_now = rotate(qkv[:, 1], positions).astype(jnp.bfloat16)
    values_now = qkv[:, 2].astype(jnp.bfloat16)
    keys_old = cache_kv[0].reshape(CACHE, HEADS, HEAD)
    values_old = cache_kv[1].reshape(CACHE, HEADS, HEAD)
    heads_out = lax.map(one_head, (jnp.transpose(queries, (1, 0, 2)), jnp.transpose(keys_now, (1, 0, 2)), jnp.transpose(values_now, (1, 0, 2)), jnp.transpose(keys_old, (1, 0, 2)), jnp.transpose(values_old, (1, 0, 2))))
    heads_out = jnp.transpose(heads_out, (1, 0, 2)).reshape(BLOCK, D)
    attended = jnp.dot(heads_out, w_out, preferred_element_type=jnp.float32)
    mixed = (wide + attended).astype(jnp.bfloat16)
    block_spectrum = jnp.stack([real_part, imag_part])
    return (mixed, block_spectrum)
```

```python
import math

import jax
import jax.numpy as jnp
from jax import lax
from jax.sharding import PartitionSpec as P

HEAD = 128


highest = lax.Precision.HIGHEST


def wave(count_a, count_b, modulus):
    first = lax.broadcasted_iota(jnp.int32, (count_a, count_b), 0)
    second = lax.broadcasted_iota(jnp.int32, (count_a, count_b), 1)
    angles = 2.0 * math.pi / modulus * (first * second % modulus).astype(jnp.float32)
    return (jnp.cos(angles), jnp.sin(angles))


def split_table(table):
    leading = table.astype(jnp.bfloat16)
    remainder = table - lax.optimization_barrier(leading).astype(jnp.float32)
    middle = remainder.astype(jnp.bfloat16)
    trailing = (remainder - lax.optimization_barrier(middle).astype(jnp.float32)).astype(
        jnp.bfloat16
    )
    return (leading, middle, trailing)


def rotate(values, positions):
    half = values.shape[-1] // 2
    freqs = 10000.0 ** (-jnp.arange(half, dtype=jnp.float32) / half)
    angles = positions.astype(jnp.float32)[:, None] * freqs[None, :]
    cosine = jnp.cos(angles)[:, None, :]
    sine = jnp.sin(angles)[:, None, :]
    first = values[..., :half]
    second = values[..., half:]
    return jnp.concatenate(
        [first * cosine - second * sine, first * sine + second * cosine], axis=-1
    )


def forward_transform(signal):
    chans, length = signal.shape
    nfft = 2 * length
    blocks = nfft // 128
    shaped = signal.reshape(chans, 64, blocks)
    cos_one, sin_one = wave(64, 128, 128)
    table = jnp.concatenate([cos_one, -sin_one], axis=1)
    section = jnp.zeros((chans, blocks, 256), jnp.float32)
    for piece in split_table(table):
        section = section + jnp.einsum(
            "cab,ak->cbk", shaped, piece, preferred_element_type=jnp.float32
        )
    part_real = section[:, :, :128]
    part_imag = section[:, :, 128:]
    cos_tw, sin_tw = wave(blocks, 128, nfft)
    turn_real = part_real * cos_tw + part_imag * sin_tw
    turn_imag = part_imag * cos_tw - part_real * sin_tw
    cos_two, sin_two = wave(blocks, blocks // 2, blocks)
    out_real = jnp.einsum("cbk,bm->cmk", turn_real, cos_two, precision=highest) + jnp.einsum(
        "cbk,bm->cmk", turn_imag, sin_two, precision=highest
    )
    out_imag = jnp.einsum("cbk,bm->cmk", turn_imag, cos_two, precision=highest) - jnp.einsum(
        "cbk,bm->cmk", turn_real, sin_two, precision=highest
    )
    return (out_real.reshape(chans, length), out_imag.reshape(chans, length))


def inverse_transform(spec_real, spec_imag):
    chans, length = spec_real.shape
    nfft = 2 * length
    blocks = nfft // 128
    weight_bins = jnp.where(jnp.arange(length) == 0, 1.0, 2.0).astype(jnp.float32)[None, :] / nfft
    scaled_real = (spec_real * weight_bins).reshape(chans, blocks // 2, 128)
    scaled_imag = (spec_imag * weight_bins).reshape(chans, blocks // 2, 128)
    cos_two, sin_two = wave(blocks // 2, blocks, blocks)
    step_real = jnp.einsum("cmk,mj->cjk", scaled_real, cos_two, precision=highest) - jnp.einsum(
        "cmk,mj->cjk", scaled_imag, sin_two, precision=highest
    )
    step_imag = jnp.einsum("cmk,mj->cjk", scaled_real, sin_two, precision=highest) + jnp.einsum(
        "cmk,mj->cjk", scaled_imag, cos_two, precision=highest
    )
    cos_tw, sin_tw = wave(blocks, 128, nfft)
    turn_real = step_real * cos_tw - step_imag * sin_tw
    turn_imag = step_real * sin_tw + step_imag * cos_tw
    cos_one, sin_one = wave(128, 64, 128)
    result = jnp.einsum("cjk,kt->ctj", turn_real, cos_one, precision=highest) - jnp.einsum(
        "cjk,kt->ctj", turn_imag, sin_one, precision=highest
    )
    return result.reshape(chans, length)


QUADS = [[2 * k, 2 * k + 1, 8 + 2 * k, 9 + 2 * k] for k in range(4)]
RINGS = [list(range(8)), list(range(8, 16))]
SAME_CORE = [[8 * g + 2 * y + c for g in range(2) for y in range(4)] for c in range(2)]
OTHER_CORE = [(j, j ^ 1) for j in range(8)]
GP = ("grp", "pb")


def pieces_of(values):
    leading = values.astype(jnp.bfloat16)
    remainder = values - lax.optimization_barrier(leading).astype(jnp.float32)
    middle = remainder.astype(jnp.bfloat16)
    trailing = (remainder - lax.optimization_barrier(middle).astype(jnp.float32)).astype(jnp.bfloat16)
    return (leading, middle, trailing)


def gather_features(block):
    copies = jnp.broadcast_to(block[None], (8,) + block.shape)
    own = lax.all_to_all(copies, GP, 0, 0, axis_index_groups=SAME_CORE)
    other = lax.ppermute(own, "pb", OTHER_CORE)
    return own, other


def by_core(own, other):
    flag = lax.axis_index("pb") % 2 == 0
    first = jnp.where(flag, own, other)
    second = jnp.where(flag, other, own)
    both = jnp.stack([first, second], axis=1)
    return jnp.transpose(both, (2, 0, 1, 3)).reshape(both.shape[2], -1)


def local(hyena_proj, dskip, filters, resident, cache_kv, norm_gain, w_qkv, w_out):
    row_count = hyena_proj.shape[1]
    head_cols = w_qkv.shape[2]
    heads_here = head_cols // HEAD
    width = w_qkv.shape[0]
    ha_index = lax.axis_index("ha")
    gated = (hyena_proj[1].astype(jnp.float32) * hyena_proj[2].astype(jnp.float32)).astype(
        jnp.bfloat16
    )
    columns = lax.all_to_all(gated.T, "ha", split_axis=0, concat_axis=1, tiled=True)
    real_part, imag_part = forward_transform(columns)
    sum_real = real_part * filters[0, 0] - imag_part * filters[0, 1]
    sum_imag = real_part * filters[0, 1] + imag_part * filters[0, 0]
    for which in (1, 2):
        old_real = resident[which - 1, 0]
        old_imag = resident[which - 1, 1]
        sum_real = sum_real + old_real * filters[which, 0] - old_imag * filters[which, 1]
        sum_imag = sum_imag + old_real * filters[which, 1] + old_imag * filters[which, 0]
    conv_cols = inverse_transform(sum_real, sum_imag).astype(jnp.bfloat16)
    conv = lax.all_to_all(conv_cols, "ha", split_axis=1, concat_axis=0, tiled=True).T
    hyena_out = (
        hyena_proj[0].astype(jnp.float32)
        * (conv.astype(jnp.float32) + dskip * gated.astype(jnp.float32))
    ).astype(jnp.bfloat16)
    whole = by_core(*gather_features(hyena_out)).astype(jnp.float32)
    meansq = jnp.mean(whole * whole, axis=1, keepdims=True)
    normed = (whole * lax.rsqrt(meansq + 1e-05) * norm_gain).astype(jnp.bfloat16)
    qkv = jnp.dot(normed, w_qkv.reshape(width, 3 * head_cols), preferred_element_type=jnp.float32)
    qkv = qkv.reshape(row_count, 3, heads_here, HEAD)
    cache_len = 16 * row_count
    local_rows = ha_index * row_count + jnp.arange(row_count, dtype=jnp.int32)
    queries = rotate(qkv[:, 0], cache_len + local_rows).astype(jnp.bfloat16)
    keys_now = rotate(qkv[:, 1], cache_len + local_rows).astype(jnp.bfloat16)
    values_now = qkv[:, 2].astype(jnp.bfloat16)
    half = ha_index // 8
    quarter = (ha_index % 8) // 2
    to_ring = jnp.transpose(queries, (1, 0, 2))
    to_ring = jnp.broadcast_to(to_ring[None], (4,) + to_ring.shape).reshape(8, row_count, HEAD)
    q_all = lax.all_to_all(to_ring, "ha", 0, 0, axis_index_groups=RINGS).reshape(8 * row_count, HEAD)

    def spread(keys, values):
        both = jnp.stack([jnp.transpose(keys, (1, 0, 2)), jnp.transpose(values, (1, 0, 2))], axis=1)
        both = jnp.broadcast_to(both[None], (2,) + both.shape).reshape(4, 2, row_count, HEAD)
        both = lax.all_to_all(both, "ha", 0, 0, axis_index_groups=QUADS)
        return both[:, 0].reshape(-1, HEAD), both[:, 1].reshape(-1, HEAD)

    cache = cache_kv.reshape(2, row_count, heads_here, HEAD)
    k_old, v_old = spread(cache[0], cache[1])
    k_new, v_new = spread(keys_now, values_now)
    keys = jnp.concatenate([k_old, k_new])
    values = jnp.concatenate([v_old, v_new])
    blocks = 2 * quarter + jnp.array([0, 1, 8, 9], jnp.int32)
    key_rows = (blocks[:, None] * row_count + jnp.arange(row_count, dtype=jnp.int32)[None]).reshape(-1)
    key_rows = jnp.concatenate([jnp.full((4 * row_count,), -1, jnp.int32), key_rows])
    query_rows = half * 8 * row_count + jnp.arange(8 * row_count, dtype=jnp.int32)
    allowed = key_rows[:, None] <= query_rows[None, :]
    scores = jnp.einsum("kd,qd->kq", keys, q_all, preferred_element_type=jnp.float32) / jnp.sqrt(
        jnp.float32(HEAD)
    )
    scores = jnp.where(allowed, scores, jnp.float32(-1e30))
    top = jnp.max(scores, axis=0)
    expd = jnp.exp(scores - top[None])
    total = jnp.sum(expd, axis=0)
    partial = jnp.einsum(
        "kd,kq->dq", values, expd.astype(jnp.bfloat16), preferred_element_type=jnp.float32
    )
    partial = (partial / total[None]).astype(jnp.bfloat16)
    level = jnp.stack(pieces_of(top + jnp.log(total)))
    sent = jnp.concatenate([partial, level, jnp.zeros((13, 8 * row_count), jnp.bfloat16)])
    sent = jnp.transpose(sent.reshape(HEAD + 16, 8, row_count), (1, 0, 2))
    got = lax.all_to_all(sent, "ha", 0, 0, axis_index_groups=RINGS).astype(jnp.float32)
    got = got.reshape(4, 2, HEAD + 16, row_count)
    level = got[:, :, HEAD] + got[:, :, HEAD + 1] + got[:, :, HEAD + 2]
    share = jnp.exp(level - jnp.max(level, axis=0))
    share = share / jnp.sum(share, axis=0)
    heads_out = jnp.sum(got[:, :, :HEAD] * share[:, :, None], axis=0)
    heads_out = heads_out.reshape(head_cols, row_count).T.astype(jnp.bfloat16)
    attended = jnp.dot(
        by_core(*gather_features(heads_out)), w_out, preferred_element_type=jnp.float32
    )
    mixed = (hyena_out.astype(jnp.float32) + attended).astype(jnp.bfloat16)
    block_spectrum = jnp.stack([real_part, imag_part])
    return (mixed, block_spectrum)


def solution(mesh):
    return jax.shard_map(
        local,
        mesh=mesh,
        in_specs=(
            P(None, "ha", ("grp", "pb")),
            P(("grp", "pb")),
            P(None, None, ("grp", "pb", "ha"), None),
            P(None, None, ("grp", "pb", "ha"), None),
            P(None, "ha", ("grp", "pb")),
            P(),
            P(None, None, ("grp", "pb")),
            P(None, ("grp", "pb")),
        ),
        out_specs=(P("ha", ("grp", "pb")), P(None, ("grp", "pb", "ha"), None)),
        check_vma=False,
    )
```

```python
import functools
import math

import jax
import jax.numpy as jnp
import ml_dtypes
import numpy as np
from jax import lax
from jax.experimental import pallas as pl
from jax.experimental.pallas import tpu as pltpu
from jax.sharding import PartitionSpec as P

HEAD = 128
BF = jnp.bfloat16
F32 = jnp.float32
GP = ("grp", "pb")
QUADS = [[2 * k, 2 * k + 1, 8 + 2 * k, 9 + 2 * k] for k in range(4)]
RINGS = [list(range(8)), list(range(8, 16))]
SAME_CORE = [[8 * g + 2 * y + c for g in range(2) for y in range(4)] for c in range(2)]
OTHER_CORE = [(j, j ^ 1) for j in range(8)]
SMEM = pl.BlockSpec(memory_space=pltpu.SMEM)


def params(mib):
    return pltpu.CompilerParams(vmem_limit_bytes=mib * 2**20)


def pair(table):
    high = table.astype(ml_dtypes.bfloat16)
    low = (table - high.astype(np.float64)).astype(ml_dtypes.bfloat16)
    return high, low


@functools.cache
def tables():
    s, k1, t = np.arange(16), np.arange(32), np.arange(256)
    eye = np.eye(16)
    angle = 2 * np.pi / 32 * (np.outer(k1, s) % 32)
    first = np.stack([np.cos(angle), -np.sin(angle)])
    first = np.einsum("rks,cd->rcksd", first, eye).reshape(1024, 256)
    angle = 2 * np.pi / 8192 * np.outer(k1, t)
    turn = np.stack([np.cos(angle), np.sin(angle)]).astype(np.float32)
    k2 = (4 * np.arange(32)[None, :] + np.arange(4)[:, None]).reshape(-1)
    angle = 2 * np.pi / 256 * (np.outer(t, k2) % 256)
    cos, sin = np.cos(angle), np.sin(angle)
    second = np.block([[cos, -sin], [sin, cos]])
    return (
        np.stack(pair(first)),
        np.stack(pair(second)),
        np.stack(pair(second.T.copy())),
        np.stack(pair(first.T.copy() / 4096.0)),
        turn,
    )


def split(values):
    high = values.astype(BF)
    return high, (values - high.astype(F32)).astype(BF)


def mul(a, b):
    return jnp.dot(a, b, preferred_element_type=F32)


def gate_kernel(proj_ref, out_ref):
    gated = (proj_ref[1].astype(F32) * proj_ref[2].astype(F32)).astype(BF).astype(F32)
    out_ref[...] = gated.T.astype(BF)


def to_tiles(nat):
    out = []
    cube = nat.reshape(16, 32, 128)
    for g in range(4):
        tile = cube[4 * g : 4 * g + 4].reshape(128, 128).T
        for c in range(4):
            out.append(
                jnp.concatenate(
                    [tile[32 * q : 32 * q + 32, 32 * c : 32 * c + 32] for q in range(4)], axis=1
                )
            )
    return jnp.concatenate(out, axis=0)


def from_tiles(tiles):
    out = []
    for g in range(4):
        part = tiles[128 * g : 128 * g + 128]
        swapped = jnp.concatenate(
            [
                jnp.concatenate(
                    [part[32 * c : 32 * c + 32, 32 * q : 32 * q + 32] for c in range(4)], axis=1
                )
                for q in range(4)
            ],
            axis=0,
        )
        out.append(swapped.T.reshape(4, 32, 128))
    return jnp.concatenate(out, axis=0).reshape(16, 4096)


def prepare_kernel(filters_ref, resident_ref, out_ref):
    lane = lax.broadcasted_iota(jnp.int32, (512, 128), 1)
    row = lax.broadcasted_iota(jnp.int32, (512, 128), 0)
    weight = jnp.where((lane == 0) & (row % 32 == 0), 0.5, 1.0)
    real = jnp.zeros((16, 4096), F32)
    imag = jnp.zeros((16, 4096), F32)
    for m in range(2):
        ar, ai = resident_ref[m, 0], resident_ref[m, 1]
        br, bi = filters_ref[m + 1, 0], filters_ref[m + 1, 1]
        real = real + ar * br - ai * bi
        imag = imag + ar * bi + ai * br
    out_ref[0] = to_tiles(filters_ref[0, 0]) * weight
    out_ref[1] = to_tiles(filters_ref[0, 1]) * weight
    out_ref[2] = to_tiles(real) * weight
    out_ref[3] = to_tiles(imag) * weight


def restore_kernel(tiles_ref, out_ref):
    out_ref[0] = from_tiles(tiles_ref[0])
    out_ref[1] = from_tiles(tiles_ref[1])


def conv_kernel(x_ref, prep_ref, first_ref, second_ref, third_ref, fourth_ref, turn_ref, conv_ref, spec_ref):
    x = x_ref[...]
    part = mul(first_ref[0], x) + mul(first_ref[1], x)
    cos, sin = turn_ref[0], turn_ref[1]
    real = part[:512].reshape(16, 32, 256)
    imag = part[512:].reshape(16, 32, 256)
    turned = jnp.concatenate(
        [(real * cos + imag * sin).reshape(512, 256), (imag * cos - real * sin).reshape(512, 256)], axis=1
    )
    high, low = split(turned)
    spec = mul(high, second_ref[0]) + mul(low, second_ref[0]) + mul(high, second_ref[1])
    real, imag = spec[:, :128], spec[:, 128:]
    spec_ref[0] = real
    spec_ref[1] = imag
    z = jnp.concatenate(
        [
            real * prep_ref[0] - imag * prep_ref[1] + prep_ref[2],
            real * prep_ref[1] + imag * prep_ref[0] + prep_ref[3],
        ],
        axis=1,
    )
    high, low = split(z)
    back = mul(high, third_ref[0]) + mul(low, third_ref[0]) + mul(high, third_ref[1])
    real = back[:, :256].reshape(16, 32, 256)
    imag = back[:, 256:].reshape(16, 32, 256)
    turned = jnp.concatenate(
        [(real * cos - imag * sin).reshape(512, 256), (real * sin + imag * cos).reshape(512, 256)], axis=0
    )
    high, low = split(turned)
    conv = mul(fourth_ref[0], high) + mul(fourth_ref[0], low) + mul(fourth_ref[1], high)
    conv_ref[...] = conv.astype(BF)


def hyena_kernel(conv_ref, proj_ref, dskip_ref, out_ref):
    conv = conv_ref[...].astype(F32).T
    gated = (proj_ref[1].astype(F32) * proj_ref[2].astype(F32)).astype(BF).astype(F32)
    value = (proj_ref[0].astype(F32) * (conv + dskip_ref[...] * gated)).astype(BF)
    for copy in range(8):
        out_ref[copy] = value


def qkv_kernel(core_ref, own_ref, other_ref, w_ref, gain_ref, turn_ref, q_ref, kv_ref, acc_ref, square_ref):
    step = pl.program_id(0)
    core = core_ref[0]

    @pl.when(step == 0)
    def _():
        acc_ref[...] = jnp.zeros_like(acc_ref)
        square_ref[...] = jnp.zeros_like(square_ref)

    for x_ref, which in ((own_ref, core), (other_ref, 1 - core)):
        x = x_ref[0].astype(F32)
        square_ref[...] += jnp.sum(x * x, axis=1, keepdims=True)
        scaled = (x * gain_ref[0, which]).astype(BF)
        for part in range(3):
            acc_ref[part] += mul(scaled, w_ref[part, 0, which])

    @pl.when(step == 7)
    def _():
        scale = lax.rsqrt(square_ref[...] / 4096.0 + 1e-05)
        cos, sin = turn_ref[0], turn_ref[1]
        for h in range(2):
            cols = slice(128 * h, 128 * h + 128)
            q = acc_ref[0, :, cols] * scale
            k = acc_ref[1, :, cols] * scale
            v = (acc_ref[2, :, cols] * scale).astype(BF)
            q = (q * cos + pltpu.roll(q, 64, 1) * sin).astype(BF)
            k = (k * cos + pltpu.roll(k, 64, 1) * sin).astype(BF)
            for dest in range(4):
                q_ref[2 * dest + h] = q
            for dest in range(2):
                kv_ref[2 * dest + h, 0] = k
                kv_ref[2 * dest + h, 1] = v


def attend_kernel(place_ref, q_ref, old_ref, new_ref, out_ref, keys_ref, values_ref):
    half, quarter = place_ref[0], place_ref[1]
    for b in range(4):
        rows = slice(256 * b, 256 * b + 256)
        later = slice(1024 + 256 * b, 1280 + 256 * b)
        keys_ref[rows] = old_ref[b, 0]
        keys_ref[later] = new_ref[b, 0]
        values_ref[:, rows] = old_ref[b, 1].astype(F32).T.astype(BF)
        values_ref[:, later] = new_ref[b, 1].astype(F32).T.astype(BF)
    unit = math.log2(math.e) / math.sqrt(HEAD)
    sub = lax.broadcasted_iota(jnp.int32, (256, 256), 0)
    lane = lax.broadcasted_iota(jnp.int32, (256, 256), 1)
    row16 = lax.broadcasted_iota(jnp.int32, (16, 256), 0)

    def tile(i, used):
        q = q_ref[i]
        count = 1024 + 256 * used
        scores = lax.dot_general(
            keys_ref[:count], q, (((1,), (1,)), ((), ())), preferred_element_type=F32
        )
        if used:
            block = 2 * quarter + (0, 1, 8, 9)[used - 1]
            ahead = (block - (8 * half + i)) * 256
            last = jnp.where(sub + ahead <= lane, scores[count - 256 :], -1e30)
            scores = jnp.concatenate([scores[: count - 256], last], axis=0)
        top = jnp.max(scores, axis=0, keepdims=True)
        expd = jnp.exp2((scores - top) * unit)
        total = jnp.sum(expd, axis=0, keepdims=True)
        part = mul(values_ref[:, :count], expd.astype(BF))
        out_ref[i, :128] = (part / total).astype(BF)
        level = top * unit + jnp.log2(total)
        a = level.astype(BF).astype(F32)
        b = (level - a).astype(BF).astype(F32)
        c = (level - a - b).astype(BF).astype(F32)
        rows = jnp.where(row16 == 0, a, jnp.where(row16 == 1, b, jnp.where(row16 == 2, c, 0.0)))
        out_ref[i, 128:] = rows.astype(BF)

    def body(i, carry):
        mine = 8 * half + i
        used = sum(jnp.where(2 * quarter + off <= mine, 1, 0) for off in (0, 1, 8, 9))
        for n in range(5):
            pl.when(used == n)(functools.partial(tile, i, n))
        return carry

    lax.fori_loop(0, 8, body, 0)


def combine_kernel(got_ref, out_ref):
    outs = []
    for h in range(2):
        levels = [
            jnp.sum(got_ref[2 * k + h, 128:].astype(F32), axis=0, keepdims=True) for k in range(4)
        ]
        top = jnp.maximum(jnp.maximum(levels[0], levels[1]), jnp.maximum(levels[2], levels[3]))
        shares = [jnp.exp2(level - top) for level in levels]
        total = shares[0] + shares[1] + shares[2] + shares[3]
        acc = jnp.zeros((128, 256), F32)
        for k in range(4):
            acc = acc + got_ref[2 * k + h, :128].astype(F32) * (shares[k] / total)
        outs.append(acc.T)
    value = jnp.concatenate(outs, axis=1).astype(BF)
    for copy in range(8):
        out_ref[copy] = value


def output_kernel(core_ref, own_ref, other_ref, w_ref, hyena_ref, out_ref, acc_ref):
    step = pl.program_id(0)
    core = core_ref[0]

    @pl.when(step == 0)
    def _():
        acc_ref[...] = hyena_ref[...].astype(F32)

    acc_ref[...] += mul(own_ref[0], w_ref[0, core]) + mul(other_ref[0], w_ref[0, 1 - core])

    @pl.when(step == 7)
    def _():
        out_ref[...] = acc_ref[...].astype(BF)


def shape(*dims, dtype=BF):
    return jax.ShapeDtypeStruct(dims, dtype)


def gather_features(copies):
    own = lax.all_to_all(copies, GP, 0, 0, axis_index_groups=SAME_CORE)
    return own, lax.ppermute(own, "pb", OTHER_CORE)


def rotation(rows, ha_index):
    freqs = 10000.0 ** (-jnp.arange(64, dtype=F32) / 64)
    places = 16 * rows + ha_index * rows + jnp.arange(rows, dtype=jnp.int32)
    angles = places.astype(F32)[:, None] * freqs[None, :]
    cos, sin = jnp.cos(angles), jnp.sin(angles)
    return jnp.stack([jnp.concatenate([cos, cos], 1), jnp.concatenate([-sin, sin], 1)])


def local(hyena_proj, dskip, filters, resident, cache_kv, norm_gain, w_qkv, w_out):
    ha_index = lax.axis_index("ha")
    core = (lax.axis_index("pb") % 2).astype(jnp.int32).reshape(1)
    place = jnp.stack([ha_index // 8, (ha_index % 8) // 2]).astype(jnp.int32)

    gated_t = pl.pallas_call(gate_kernel, out_shape=shape(256, 256), name="gate")(hyena_proj)
    columns = lax.all_to_all(gated_t.reshape(16, 16, 256), "ha", 0, 0).reshape(256, 256)
    prep = pl.pallas_call(
        prepare_kernel, out_shape=shape(4, 512, 128, dtype=F32), name="prepare", compiler_params=params(24)
    )(filters, resident)
    conv, tiles = pl.pallas_call(
        conv_kernel,
        out_shape=(shape(256, 256), shape(2, 512, 128, dtype=F32)),
        name="convolve",
        compiler_params=params(32),
    )(columns, prep, *(jnp.asarray(t) for t in tables()))
    conv = lax.all_to_all(conv.reshape(16, 16, 256), "ha", 0, 0).reshape(256, 256)
    block_spectrum = pl.pallas_call(
        restore_kernel, out_shape=shape(2, 16, 4096, dtype=F32), name="restore", compiler_params=params(24)
    )(tiles)
    copies = pl.pallas_call(hyena_kernel, out_shape=shape(8, 256, 256), name="hyena")(
        conv, hyena_proj, dskip.reshape(1, 256)
    )
    own, other = gather_features(copies)

    block = pl.BlockSpec((1, 256, 256), lambda s: (s, 0, 0))
    q_msg, kv_msg = pl.pallas_call(
        qkv_kernel,
        grid=(8,),
        in_specs=[
            SMEM,
            block,
            block,
            pl.BlockSpec((3, 1, 2, 256, 256), lambda s: (0, s, 0, 0, 0)),
            pl.BlockSpec((1, 2, 1, 256), lambda s: (s, 0, 0, 0)),
            pl.BlockSpec((2, 256, 128), lambda s: (0, 0, 0)),
        ],
        out_specs=[
            pl.BlockSpec((8, 256, 128), lambda s: (0, 0, 0)),
            pl.BlockSpec((4, 2, 256, 128), lambda s: (0, 0, 0, 0)),
        ],
        out_shape=(shape(8, 256, 128), shape(4, 2, 256, 128)),
        scratch_shapes=[pltpu.VMEM((3, 256, 256), F32), pltpu.VMEM((256, 1), F32)],
        name="project",
        compiler_params=params(24),
    )(
        core,
        own,
        other,
        jnp.transpose(w_qkv, (1, 0, 2)).reshape(3, 8, 2, 256, 256),
        norm_gain.reshape(8, 2, 1, 256),
        rotation(256, ha_index),
    )

    cache = jnp.transpose(cache_kv.reshape(2, 256, 2, 128), (2, 0, 1, 3))
    cache = jnp.broadcast_to(cache[None], (2, 2, 2, 256, 128)).reshape(4, 2, 256, 128)
    old = lax.all_to_all(cache, "ha", 0, 0, axis_index_groups=QUADS)
    queries = lax.all_to_all(q_msg, "ha", 0, 0, axis_index_groups=RINGS)
    new = lax.all_to_all(kv_msg, "ha", 0, 0, axis_index_groups=QUADS)
    partial = pl.pallas_call(
        attend_kernel,
        in_specs=[SMEM] + [pl.BlockSpec()] * 3,
        out_shape=shape(8, 144, 256),
        scratch_shapes=[pltpu.VMEM((2048, 128), BF), pltpu.VMEM((128, 2048), BF)],
        name="attend",
        compiler_params=params(24),
    )(place, queries, old, new)
    got = lax.all_to_all(partial, "ha", 0, 0, axis_index_groups=RINGS)
    copies_out = pl.pallas_call(combine_kernel, out_shape=shape(8, 256, 256), name="combine")(got)
    own, other = gather_features(copies_out)
    mixed = pl.pallas_call(
        output_kernel,
        grid=(8,),
        in_specs=[
            SMEM,
            block,
            block,
            pl.BlockSpec((1, 2, 256, 256), lambda s: (s, 0, 0, 0)),
            pl.BlockSpec((None, 256, 256), lambda s: (0, 0, 0)),
        ],
        out_specs=pl.BlockSpec((256, 256), lambda s: (0, 0)),
        out_shape=shape(256, 256),
        scratch_shapes=[pltpu.VMEM((256, 256), F32)],
        name="output",
        compiler_params=params(16),
    )(core, own, other, w_out.reshape(8, 2, 256, 256), copies)
    return (mixed, block_spectrum)


def solution(mesh):
    return jax.shard_map(
        local,
        mesh=mesh,
        in_specs=(
            P(None, "ha", ("grp", "pb")),
            P(("grp", "pb")),
            P(None, None, ("grp", "pb", "ha"), None),
            P(None, None, ("grp", "pb", "ha"), None),
            P(None, "ha", ("grp", "pb")),
            P(),
            P(None, None, ("grp", "pb")),
            P(None, ("grp", "pb")),
        ),
        out_specs=(P("ha", ("grp", "pb")), P(None, ("grp", "pb", "ha"), None)),
        check_vma=False,
    )
```

```python
import functools
import math

import jax
import jax.numpy as jnp
import ml_dtypes
import numpy as np
from jax import lax
from jax.experimental import pallas as pl
from jax.experimental.pallas import tpu as pltpu
from jax.sharding import PartitionSpec as P

HEAD = 128
BF = jnp.bfloat16
F32 = jnp.float32
GP = ("grp", "pb")
NEAR = [[8 * x + k for x in range(2) for k in range(4)], [8 * x + 7 - k for x in range(2) for k in range(4)]]
SAME_CORE = [[8 * g + 2 * y + c for g in range(2) for y in range(4)] for c in range(2)]
OTHER_CORE = [(j, j ^ 1) for j in range(8)]
SMEM = pl.BlockSpec(memory_space=pltpu.SMEM)


def params(mib):
    return pltpu.CompilerParams(vmem_limit_bytes=mib * 2**20)


def pair(table):
    high = table.astype(ml_dtypes.bfloat16)
    low = (table - high.astype(np.float64)).astype(ml_dtypes.bfloat16)
    return high, low


@functools.cache
def tables():
    s, k1, t = np.arange(16), np.arange(32), np.arange(256)
    eye = np.eye(16)
    angle = 2 * np.pi / 32 * (np.outer(k1, s) % 32)
    compact = np.stack([np.cos(angle), -np.sin(angle)])
    first = np.einsum("rks,cd->rcksd", compact, eye).reshape(1024, 256)
    angle = 2 * np.pi / 8192 * np.outer(k1, t)
    turn = np.stack([np.cos(angle), np.sin(angle)])
    k2 = (4 * np.arange(32)[None, :] + np.arange(4)[:, None]).reshape(-1)
    angle = 2 * np.pi / 256 * (np.outer(t, k2) % 256)
    cos, sin = np.cos(angle), np.sin(angle)
    second = np.block([[cos, -sin], [sin, cos]])
    compact = np.repeat(compact.reshape(64, 16), 16, axis=1)
    fourth = (first.T / 4096.0).reshape(256, 4, 256).transpose(1, 0, 2).reshape(1024, 256)
    rows = [part for table in (compact, turn.reshape(64, 256), second, fourth) for part in pair(table)]
    return np.concatenate(rows)


def split(values):
    high = values.astype(BF)
    return high, (values - high.astype(F32)).astype(BF)


def mul(a, b):
    return jnp.dot(a, b, preferred_element_type=F32)


def mul_t(a, b):
    return lax.dot_general(a, b, (((1,), (1,)), ((), ())), preferred_element_type=F32)


def gate_kernel(proj_ref, turned_ref):
    gated = (proj_ref[1].astype(F32) * proj_ref[2].astype(F32)).astype(BF)
    turned_ref[...] = gated.astype(F32).T.astype(BF)


def to_tiles(nat):
    out = []
    cube = nat.reshape(16, 32, 128)
    for g in range(4):
        tile = cube[4 * g : 4 * g + 4].reshape(128, 128).T
        for c in range(4):
            out.append(
                jnp.concatenate(
                    [tile[32 * q : 32 * q + 32, 32 * c : 32 * c + 32] for q in range(4)], axis=1
                )
            )
    return jnp.concatenate(out, axis=0)


def from_tiles(tiles):
    out = []
    for g in range(4):
        part = tiles[128 * g : 128 * g + 128]
        swapped = jnp.concatenate(
            [
                jnp.concatenate(
                    [part[32 * c : 32 * c + 32, 32 * q : 32 * q + 32] for c in range(4)], axis=1
                )
                for q in range(4)
            ],
            axis=0,
        )
        out.append(swapped.T.reshape(4, 32, 128))
    return jnp.concatenate(out, axis=0).reshape(16, 4096)


def prepare_kernel(filters_ref, resident_ref, proj_ref, out_ref, outer_ref, gated_ref):
    outer_ref[...] = proj_ref[0]
    gated_ref[...] = (proj_ref[1].astype(F32) * proj_ref[2].astype(F32)).astype(BF)
    lane = lax.broadcasted_iota(jnp.int32, (512, 128), 1)
    row = lax.broadcasted_iota(jnp.int32, (512, 128), 0)
    weight = jnp.where((lane == 0) & (row % 32 == 0), 0.5, 1.0)
    real = jnp.zeros((16, 4096), F32)
    imag = jnp.zeros((16, 4096), F32)
    for m in range(2):
        ar, ai = resident_ref[m, 0], resident_ref[m, 1]
        br, bi = filters_ref[m + 1, 0], filters_ref[m + 1, 1]
        real = real + ar * br - ai * bi
        imag = imag + ar * bi + ai * br
    out_ref[0] = to_tiles(filters_ref[0, 0]) * weight
    out_ref[1] = to_tiles(filters_ref[0, 1]) * weight
    out_ref[2] = to_tiles(real) * weight
    out_ref[3] = to_tiles(imag) * weight


def restore_kernel(tiles_ref, after_ref, out_ref, token_ref):
    token_ref[...] = jnp.zeros_like(token_ref)
    out_ref[0] = from_tiles(tiles_ref[0])
    out_ref[1] = from_tiles(tiles_ref[1])


def conv_kernel(x_ref, prep_ref, table_ref, after_ref, conv_ref, spec_ref):
    x = x_ref[...]
    channel = lax.broadcasted_iota(jnp.int32, (2, 16, 32, 256), 1)
    lane = lax.broadcasted_iota(jnp.int32, (2, 16, 32, 256), 3)
    own = lane % 16 == channel
    part = jnp.zeros((1024, 256), F32)
    for n in range(2):
        block = table_ref[64 * n : 64 * n + 64].astype(F32).reshape(2, 1, 32, 256)
        block = jnp.where(own, block, 0.0).reshape(1024, 256).astype(BF)
        part = part + mul(block, x)
    turn = table_ref[128:192].astype(F32) + table_ref[192:256].astype(F32)
    cos, sin = turn[:32], turn[32:]
    second = [table_ref[256 + 512 * n : 768 + 512 * n] for n in range(2)]
    real = part[:512].reshape(16, 32, 256)
    imag = part[512:].reshape(16, 32, 256)
    turned = jnp.concatenate(
        [(real * cos + imag * sin).reshape(512, 256), (imag * cos - real * sin).reshape(512, 256)], axis=1
    )
    high, low = split(turned)
    spec = mul(high, second[0]) + mul(low, second[0]) + mul(high, second[1])
    real, imag = spec[:, :128], spec[:, 128:]
    spec_ref[0] = real
    spec_ref[1] = imag
    z = jnp.concatenate(
        [
            real * prep_ref[0] - imag * prep_ref[1] + prep_ref[2],
            real * prep_ref[1] + imag * prep_ref[0] + prep_ref[3],
        ],
        axis=1,
    )
    high, low = split(z)
    back = mul_t(high, second[0]) + mul_t(low, second[0]) + mul_t(high, second[1])
    real = back[:, :256].reshape(16, 32, 256)
    imag = back[:, 256:].reshape(16, 32, 256)
    turned = jnp.concatenate(
        [(real * cos - imag * sin).reshape(512, 256), (real * sin + imag * cos).reshape(512, 256)], axis=0
    )
    high, low = split(turned)
    fourth = [
        jnp.concatenate([table_ref[1280 + 1024 * n + 256 * j : 1536 + 1024 * n + 256 * j] for j in range(4)], axis=1)
        for n in range(2)
    ]
    conv = mul(fourth[0], high) + mul(fourth[0], low) + mul(fourth[1], high)
    conv_ref[...] = conv.astype(BF)


def hyena_kernel(conv_ref, gated_ref, outer_ref, dskip_ref, out_ref, value_ref):
    conv = conv_ref[...].astype(F32).T
    value = outer_ref[...].astype(F32) * (conv + dskip_ref[...] * gated_ref[...].astype(F32))
    value = value.astype(BF)
    value_ref[...] = value
    for copy in range(8):
        out_ref[copy] = value


def pick_kernel(place_ref, cache_ref, after_ref, mine_ref, theirs_ref):
    own = place_ref[0]
    for ref, head in ((mine_ref, own), (theirs_ref, 1 - own)):
        ref[...] = cache_ref[:, :, pl.ds(pl.multiple_of(head * HEAD, HEAD), HEAD)]


def rotated(values, cos, sin):
    return values * cos + pltpu.roll(values, 64, 1) * sin


def qkv_kernel(
    place_ref, own_ref, other_ref, w_ref, gain_ref, turn_ref, token_ref,
    q_ref, scale_ref, mine_ref, theirs_ref, acc_ref, square_ref,
):
    step = pl.program_id(0)
    own_head, core = place_ref[0], place_ref[3]

    @pl.when(step == 0)
    def _():
        acc_ref[...] = jnp.zeros_like(acc_ref)
        square_ref[...] = jnp.zeros_like(square_ref)

    a, b = own_ref[0].astype(F32), other_ref[0].astype(F32)
    square_ref[...] += a * a + b * b
    a = (a * gain_ref[2 * step + core]).astype(BF)
    b = (b * gain_ref[2 * step + 1 - core]).astype(BF)
    for part in range(3):
        acc_ref[part] += mul(a, w_ref[part, 0, core]) + mul(b, w_ref[part, 0, 1 - core])

    @pl.when(step == 7)
    def _():
        scale = lax.rsqrt(jnp.sum(square_ref[...], axis=1, keepdims=True) / 4096.0 + 1e-05)
        cos, sin = turn_ref[0], turn_ref[1]
        q_ref[...] = acc_ref[0]
        scale_ref[...] = jnp.broadcast_to(scale, (256, 128))
        first = own_head == 0
        for slot in range(2):
            low, high = (acc_ref[slot + 1, :, 128 * h : 128 * h + 128] * scale for h in range(2))
            mine = jnp.where(first, low, high)
            theirs = jnp.where(first, high, low)
            if slot == 0:
                mine = rotated(mine, cos, sin)
                theirs = rotated(theirs, cos, sin)
            mine_ref[slot] = mine.astype(BF)
            theirs_ref[slot] = theirs.astype(BF)


def queries_kernel(raw_ref, scale_ref, turn_ref, q_ref):
    scale = scale_ref[...] * (math.log2(math.e) / math.sqrt(HEAD))
    for h in range(2):
        q = raw_ref[:, 128 * h : 128 * h + 128] * scale
        q = rotated(q, turn_ref[0], turn_ref[1]).astype(BF)
        for dest in range(4):
            q_ref[4 * h + dest] = q


def stage_kernel(*refs):
    keys_ref, values_ref = refs[4:]
    for n, piece in enumerate(refs[:4]):
        keys_ref[256 * n : 256 * n + 256] = piece[0]
        values_ref[:, 256 * n : 256 * n + 256] = piece[1].astype(F32).T.astype(BF)


def attend_kernel(place_ref, q_ref, keys_ref, values_ref, *rest):
    pieces, (out_ref, new_keys, new_values) = rest[:4], rest[4:]
    x, q, k = place_ref[0], place_ref[1], place_ref[2]
    slots = (2 * x + q, 2 * x + 1 - q, 2 * (1 - x) + q, 2 * (1 - x) + 1 - q)
    for slot, piece in zip(slots, pieces):
        spot = pl.ds(pl.multiple_of(slot * 256, 256), 256)
        new_keys[spot, :] = piece[0]
        new_values[:, spot] = piece[1].astype(F32).T.astype(BF)
    sub = lax.broadcasted_iota(jnp.int32, (256, 256), 0)
    lane = lax.broadcasted_iota(jnp.int32, (256, 256), 1)
    row16 = lax.broadcasted_iota(jnp.int32, (16, 256), 0)

    def block_of(i):
        near = i % 4
        return 8 * (i // 4) + jnp.where(q == 0, near, 7 - near)

    def scores_of(i, used):
        scores = [mul_t(keys_ref[...], q_ref[i])]
        if used:
            now = mul_t(new_keys[: 256 * used], q_ref[i])
            block = (k, 7 - k, 8 + k, 15 - k)[used - 1]
            ahead = (block - block_of(i)) * 256
            last = jnp.where(sub + ahead <= lane, now[256 * used - 256 :], -1e30)
            scores += [now[: 256 * used - 256], last] if used > 1 else [last]
        return jnp.concatenate(scores, axis=0)

    def finish(i, top, total, part):
        out_ref[i, :128] = (part / total).astype(BF)
        level = top + jnp.log2(total)
        a = level.astype(BF).astype(F32)
        b = (level - a).astype(BF).astype(F32)
        c = (level - a - b).astype(BF).astype(F32)
        rows = jnp.where(row16 == 0, a, jnp.where(row16 == 1, b, jnp.where(row16 == 2, c, 0.0)))
        out_ref[i, 128:] = rows.astype(BF)

    def two(tiles, used):
        found = []
        for i, n in zip(tiles, used):
            scores = scores_of(i, n)
            found.append((scores, jnp.max(scores, axis=0, keepdims=True)))
        done = []
        for (scores, top), n in zip(found, used):
            expd = jnp.exp2(scores - top)
            total = jnp.sum(expd, axis=0, keepdims=True)
            expd = expd.astype(BF)
            part = mul(values_ref[...], expd[:1024])
            if n:
                part = part + mul(new_values[:, : 256 * n], expd[1024:])
            done.append((top, total, part))
        for i, results in zip(tiles, done):
            finish(i, *results)

    def used_by(i):
        return sum(jnp.where(block <= block_of(i), 1, 0) for block in (k, 7 - k, 8 + k, 15 - k))

    def body(j, carry):
        tiles = (2 * j + q, 2 * j + 1 - q)
        low, high = (used_by(i) for i in tiles)
        for n in range(5):
            for more in (0, 1) if n < 4 else (0,):
                pl.when((low == n) & (high == n + more))(functools.partial(two, tiles, (n, n + more)))
        return carry

    lax.fori_loop(0, 4, body, 0)


def combine_kernel(got_ref, out_ref):
    outs = []
    for h in range(2):
        levels = [
            jnp.sum(got_ref[4 * h + k, 128:].astype(F32), axis=0, keepdims=True) for k in range(4)
        ]
        top = jnp.maximum(jnp.maximum(levels[0], levels[1]), jnp.maximum(levels[2], levels[3]))
        shares = [jnp.exp2(level - top) for level in levels]
        total = shares[0] + shares[1] + shares[2] + shares[3]
        acc = jnp.zeros((128, 256), F32)
        for k in range(4):
            acc = acc + got_ref[4 * h + k, :128].astype(F32) * (shares[k] / total)
        outs.append(acc.T)
    value = jnp.concatenate(outs, axis=1).astype(BF)
    for copy in range(8):
        out_ref[copy] = value


def output_own_kernel(place_ref, own_ref, w_ref, hyena_ref, out_ref):
    core = place_ref[3]
    acc = hyena_ref[...].astype(F32)
    for s in range(8):
        acc = acc + mul(own_ref[s], w_ref[2 * s + core])
    out_ref[...] = acc


def output_kernel(place_ref, other_ref, w_ref, part_ref, out_ref):
    core = 1 - place_ref[3]
    acc = part_ref[...]
    for s in range(8):
        acc = acc + mul(other_ref[s], w_ref[2 * s + core])
    out_ref[...] = acc.astype(BF)


def shape(*dims, dtype=BF):
    return jax.ShapeDtypeStruct(dims, dtype)


def rotation(rows, ha_index):
    freqs = 10000.0 ** (-jnp.arange(64, dtype=F32) / 64)
    places = 16 * rows + ha_index * rows + jnp.arange(rows, dtype=jnp.int32)
    angles = places.astype(F32)[:, None] * freqs[None, :]
    cos, sin = jnp.cos(angles), jnp.sin(angles)
    return jnp.stack([jnp.concatenate([cos, cos], 1), jnp.concatenate([-sin, sin], 1)])


X_FLIP = [(i, i ^ 8) for i in range(16)]
Q_FLIP = [(i, i ^ 7) for i in range(16)]
XQ_FLIP = [(i, i ^ 15) for i in range(16)]


def trade(mine, theirs):
    return (
        mine,
        lax.ppermute(mine, "ha", Q_FLIP),
        lax.ppermute(theirs, "ha", X_FLIP),
        lax.ppermute(theirs, "ha", XQ_FLIP),
    )


WHOLE = pl.BlockSpec()
FAR = pl.BlockSpec(memory_space=pltpu.HBM)


def gather_same_core(copies):
    return lax.all_to_all(copies, GP, 0, 0, axis_index_groups=SAME_CORE)


def local(hyena_proj, dskip, filters, resident, cache_kv, norm_gain, w_qkv, w_out):
    ha_index = lax.axis_index("ha")
    core = lax.axis_index("pb") % 2
    z = ha_index % 8
    query_half = z // 4
    place = jnp.stack([ha_index // 8, query_half, jnp.where(query_half == 0, z, 7 - z), core]).astype(jnp.int32)

    gated_t = pl.pallas_call(
        gate_kernel, out_shape=shape(256, 256), name="gate", compiler_params=params(4)
    )(hyena_proj)
    columns = lax.all_to_all(gated_t.reshape(16, 16, 256), "ha", 0, 0).reshape(256, 256)
    turn = rotation(256, ha_index)
    prep, outer, gated = pl.pallas_call(
        prepare_kernel,
        out_shape=(shape(4, 512, 128, dtype=F32), shape(256, 256), shape(256, 256)),
        name="prepare",
        compiler_params=params(16),
    )(filters, resident, hyena_proj)
    conv, tiles = pl.pallas_call(
        conv_kernel,
        out_shape=(shape(256, 256), shape(2, 512, 128, dtype=F32)),
        in_specs=[WHOLE] * 3 + [FAR],
        name="convolve",
        compiler_params=params(24),
    )(columns, prep, jnp.asarray(tables()), turn)
    conv = lax.all_to_all(conv.reshape(16, 16, 256), "ha", 0, 0).reshape(256, 256)
    copies, hyena_out = pl.pallas_call(
        hyena_kernel,

        out_shape=(shape(8, 256, 256), shape(256, 256)),
        name="hyena",
        compiler_params=params(6),
    )(conv, gated, outer, dskip.reshape(1, 256))

    own = gather_same_core(copies)
    mine, theirs = pl.pallas_call(
        pick_kernel,
        in_specs=[SMEM, WHOLE, FAR],
        out_shape=(shape(2, 256, 128), shape(2, 256, 128)),
        name="pick",
        compiler_params=params(4),
    )(place, cache_kv, hyena_out)
    own, old = lax.optimization_barrier((own, trade(mine, theirs)))
    other = lax.ppermute(own, "pb", OTHER_CORE)
    block_spectrum, token = pl.pallas_call(
        restore_kernel,
        in_specs=[WHOLE, FAR],
        out_shape=(shape(2, 16, 4096, dtype=F32), shape(8, 128, dtype=F32)),
        name="restore",
        compiler_params=params(8),
    )(tiles, own)
    block = pl.BlockSpec((1, 256, 256), lambda s: (s, 0, 0))
    trio = lambda *dims: pl.BlockSpec(dims, lambda s: (0,) * len(dims))
    raw, scale, mine, theirs = pl.pallas_call(
        qkv_kernel,
        grid=(8,),
        in_specs=[
            SMEM,
            block,
            block,
            pl.BlockSpec((3, 1, 2, 256, 256), lambda s: (0, s, 0, 0, 0)),
            trio(16, 1, 256),
            trio(2, 256, 128),
            FAR,
        ],
        out_specs=(trio(256, 256), trio(256, 128), trio(2, 256, 128), trio(2, 256, 128)),
        out_shape=(
            shape(256, 256, dtype=F32),
            shape(256, 128, dtype=F32),
            shape(2, 256, 128),
            shape(2, 256, 128),
        ),
        scratch_shapes=[pltpu.VMEM((3, 256, 256), F32), pltpu.VMEM((256, 256), F32)],
        name="project",
        compiler_params=params(16),
    )(
        place,
        own,
        other,
        jnp.transpose(w_qkv, (1, 0, 2)).reshape(3, 8, 2, 256, 256),
        norm_gain.reshape(16, 1, 256),
        turn,
        token,
    )
    new = trade(mine, theirs)
    q_msg = pl.pallas_call(
        queries_kernel, out_shape=shape(8, 256, 128), name="queries", compiler_params=params(4)
    )(raw, scale, turn)
    queries = lax.all_to_all(q_msg, "ha", 0, 0, axis_index_groups=NEAR)
    keys, values = pl.pallas_call(
        stage_kernel, out_shape=(shape(1024, 128), shape(128, 1024)), name="stage", compiler_params=params(8)
    )(*old)
    partial = pl.pallas_call(
        attend_kernel,
        in_specs=[SMEM] + [WHOLE] * 7,
        out_shape=shape(8, 144, 256),
        scratch_shapes=[pltpu.VMEM((1024, 128), BF), pltpu.VMEM((128, 1024), BF)],
        name="attend",
        compiler_params=params(20),
    )(place, queries, keys, values, *new)
    got = lax.all_to_all(partial, "ha", 0, 0, axis_index_groups=NEAR)
    copies_out = pl.pallas_call(
        combine_kernel, out_shape=shape(8, 256, 256), name="combine", compiler_params=params(8)
    )(got)
    own = gather_same_core(copies_out)
    other = lax.ppermute(own, "pb", OTHER_CORE)
    w_blocks = w_out.reshape(16, 256, 256)
    part = pl.pallas_call(
        output_own_kernel,
        in_specs=[SMEM, WHOLE, WHOLE, WHOLE],
        out_shape=shape(256, 256, dtype=F32),
        name="output_own",
        compiler_params=params(8),
    )(place, own, w_blocks, hyena_out)
    mixed = pl.pallas_call(
        output_kernel,
        in_specs=[SMEM] + [WHOLE] * 3,
        out_shape=shape(256, 256),
        name="output",
        compiler_params=params(8),
    )(place, other, w_blocks, part)
    return (mixed, block_spectrum)


def solution(mesh):
    return jax.shard_map(
        local,
        mesh=mesh,
        in_specs=(
            P(None, "ha", ("grp", "pb")),
            P(("grp", "pb")),
            P(None, None, ("grp", "pb", "ha"), None),
            P(None, None, ("grp", "pb", "ha"), None),
            P(None, "ha", ("grp", "pb")),
            P(),
            P(None, None, ("grp", "pb")),
            P(None, ("grp", "pb")),
        ),
        out_specs=(P("ha", ("grp", "pb")), P(None, ("grp", "pb", "ha"), None)),
        check_vma=False,
    )
```

```python
import functools
import math

import jax
import jax.numpy as jnp
import ml_dtypes
import numpy as np
from jax import lax
from jax.experimental import pallas as pl
from jax.experimental.pallas import tpu as pltpu
from jax.sharding import PartitionSpec as P

HEAD = 128
BF = jnp.bfloat16
F32 = jnp.float32
GP = ("grp", "pb")
NEAR = [[8 * x + k for x in range(2) for k in range(4)], [8 * x + 7 - k for x in range(2) for k in range(4)]]
SAME_CORE = [[8 * g + 2 * y + c for g in range(2) for y in range(4)] for c in range(2)]
OTHER_CORE = [(j, j ^ 1) for j in range(8)]
SMEM = pl.BlockSpec(memory_space=pltpu.SMEM)


def params(mib):
    return pltpu.CompilerParams(vmem_limit_bytes=mib * 2**20)


def pair(table):
    high = table.astype(ml_dtypes.bfloat16)
    low = (table - high.astype(np.float64)).astype(ml_dtypes.bfloat16)
    return high, low


@functools.cache
def tables():
    s, k1, t = np.arange(16), np.arange(32), np.arange(256)
    eye = np.eye(16)
    angle = 2 * np.pi / 32 * (np.outer(k1, s) % 32)
    compact = np.stack([np.cos(angle), -np.sin(angle)])
    first = np.einsum("rks,cd->rcksd", compact, eye).reshape(1024, 256)
    angle = 2 * np.pi / 8192 * np.outer(k1, t)
    turn = np.stack([np.cos(angle), np.sin(angle)])
    k2 = (4 * np.arange(32)[None, :] + np.arange(4)[:, None]).reshape(-1)
    angle = 2 * np.pi / 256 * (np.outer(t, k2) % 256)
    cos, sin = np.cos(angle), np.sin(angle)
    second = np.block([[cos, -sin], [sin, cos]])
    compact = np.repeat(compact.reshape(64, 16), 16, axis=1)
    fourth = (first.T / 4096.0).reshape(256, 4, 256).transpose(1, 0, 2).reshape(1024, 256)
    rows = [part for table in (compact, turn.reshape(64, 256), second, fourth) for part in pair(table)]
    return np.concatenate(rows)


def split(values):
    high = values.astype(BF)
    return high, (values - high.astype(F32)).astype(BF)


def mul(a, b):
    return jnp.dot(a, b, preferred_element_type=F32)


def mul_t(a, b):
    return lax.dot_general(a, b, (((1,), (1,)), ((), ())), preferred_element_type=F32)


def gate_kernel(proj_ref, turned_ref):
    gated = (proj_ref[1].astype(F32) * proj_ref[2].astype(F32)).astype(BF)
    turned_ref[...] = gated.astype(F32).T.astype(BF)


def to_tiles(nat):
    out = []
    cube = nat.reshape(16, 32, 128)
    for g in range(4):
        tile = cube[4 * g : 4 * g + 4].reshape(128, 128).T
        for c in range(4):
            out.append(
                jnp.concatenate(
                    [tile[32 * q : 32 * q + 32, 32 * c : 32 * c + 32] for q in range(4)], axis=1
                )
            )
    return jnp.concatenate(out, axis=0)


def from_tiles(tiles):
    out = []
    for g in range(4):
        part = tiles[128 * g : 128 * g + 128]
        swapped = jnp.concatenate(
            [
                jnp.concatenate(
                    [part[32 * c : 32 * c + 32, 32 * q : 32 * q + 32] for c in range(4)], axis=1
                )
                for q in range(4)
            ],
            axis=0,
        )
        out.append(swapped.T.reshape(4, 32, 128))
    return jnp.concatenate(out, axis=0).reshape(16, 4096)


def prepare_kernel(filters_ref, resident_ref, proj_ref, out_ref, outer_ref, gated_ref):
    outer_ref[...] = proj_ref[0]
    gated_ref[...] = (proj_ref[1].astype(F32) * proj_ref[2].astype(F32)).astype(BF)
    lane = lax.broadcasted_iota(jnp.int32, (512, 128), 1)
    row = lax.broadcasted_iota(jnp.int32, (512, 128), 0)
    weight = jnp.where((lane == 0) & (row % 32 == 0), 0.5, 1.0)
    real = jnp.zeros((16, 4096), F32)
    imag = jnp.zeros((16, 4096), F32)
    for m in range(2):
        ar, ai = resident_ref[m, 0], resident_ref[m, 1]
        br, bi = filters_ref[m + 1, 0], filters_ref[m + 1, 1]
        real = real + ar * br - ai * bi
        imag = imag + ar * bi + ai * br
    out_ref[0] = to_tiles(filters_ref[0, 0]) * weight
    out_ref[1] = to_tiles(filters_ref[0, 1]) * weight
    out_ref[2] = to_tiles(real) * weight
    out_ref[3] = to_tiles(imag) * weight


def restore_kernel(tiles_ref, after_ref, out_ref, token_ref):
    token_ref[...] = jnp.zeros_like(token_ref)
    out_ref[0] = from_tiles(tiles_ref[0])
    out_ref[1] = from_tiles(tiles_ref[1])


def conv_kernel(x_ref, prep_ref, table_ref, conv_ref, spec_ref):
    x = x_ref[...]
    channel = lax.broadcasted_iota(jnp.int32, (2, 16, 32, 256), 1)
    lane = lax.broadcasted_iota(jnp.int32, (2, 16, 32, 256), 3)
    own = lane % 16 == channel
    part = jnp.zeros((1024, 256), F32)
    for n in range(2):
        block = table_ref[64 * n : 64 * n + 64].astype(F32).reshape(2, 1, 32, 256)
        block = jnp.where(own, block, 0.0).reshape(1024, 256).astype(BF)
        part = part + mul(block, x)
    turn = table_ref[128:192].astype(F32) + table_ref[192:256].astype(F32)
    cos, sin = turn[:32], turn[32:]
    second = [table_ref[256 + 512 * n : 768 + 512 * n] for n in range(2)]
    real = part[:512].reshape(16, 32, 256)
    imag = part[512:].reshape(16, 32, 256)
    turned = jnp.concatenate(
        [(real * cos + imag * sin).reshape(512, 256), (imag * cos - real * sin).reshape(512, 256)], axis=1
    )
    high, low = split(turned)
    spec = mul(high, second[0]) + mul(low, second[0]) + mul(high, second[1])
    real, imag = spec[:, :128], spec[:, 128:]
    spec_ref[0] = real
    spec_ref[1] = imag
    z = jnp.concatenate(
        [
            real * prep_ref[0] - imag * prep_ref[1] + prep_ref[2],
            real * prep_ref[1] + imag * prep_ref[0] + prep_ref[3],
        ],
        axis=1,
    )
    high, low = split(z)
    back = mul_t(high, second[0]) + mul_t(low, second[0]) + mul_t(high, second[1])
    real = back[:, :256].reshape(16, 32, 256)
    imag = back[:, 256:].reshape(16, 32, 256)
    turned = jnp.concatenate(
        [(real * cos - imag * sin).reshape(512, 256), (real * sin + imag * cos).reshape(512, 256)], axis=0
    )
    high, low = split(turned)
    fourth = [
        jnp.concatenate([table_ref[1280 + 1024 * n + 256 * j : 1536 + 1024 * n + 256 * j] for j in range(4)], axis=1)
        for n in range(2)
    ]
    conv = mul(fourth[0], high) + mul(fourth[0], low) + mul(fourth[1], high)
    conv_ref[...] = conv.astype(BF)


def hyena_kernel(conv_ref, gated_ref, outer_ref, dskip_ref, out_ref, value_ref):
    conv = conv_ref[...].astype(F32).T
    value = outer_ref[...].astype(F32) * (conv + dskip_ref[...] * gated_ref[...].astype(F32))
    value = value.astype(BF)
    value_ref[...] = value
    for copy in range(8):
        out_ref[copy] = value


def pick_kernel(place_ref, cache_ref, after_ref, mine_ref, theirs_ref):
    own = place_ref[0]
    for ref, head in ((mine_ref, own), (theirs_ref, 1 - own)):
        ref[...] = cache_ref[:, :, pl.ds(pl.multiple_of(head * HEAD, HEAD), HEAD)]


def rotated(values, cos, sin):
    return values * cos + pltpu.roll(values, 64, 1) * sin


def scale_kernel(place_ref, own_ref, other_ref, gain_ref, token_ref, x_ref, scale_ref):
    core = place_ref[3]
    square = jnp.zeros((256, 256), F32)
    for s in range(8):
        for ref, which in ((own_ref, core), (other_ref, 1 - core)):
            x = ref[s].astype(F32)
            square = square + x * x
            place = 2 * s + which
            x_ref[:, pl.ds(pl.multiple_of(place * 256, 256), 256)] = (x * gain_ref[place]).astype(BF)
    scale = lax.rsqrt(jnp.sum(square, axis=1, keepdims=True) / 4096.0 + 1e-05)
    scale_ref[...] = jnp.broadcast_to(scale, (256, 128))


def qkv_kernel(place_ref, x_ref, scale_ref, w_ref, turn_ref, q_ref, mine_ref, theirs_ref):
    first = place_ref[0] == 0
    cos, sin = turn_ref[0], turn_ref[1]
    for slot in range(2):
        part = mul(x_ref[...], w_ref[slot + 1])
        low, high = (part[:, 128 * h : 128 * h + 128] * scale_ref[...] for h in range(2))
        mine = jnp.where(first, low, high)
        theirs = jnp.where(first, high, low)
        if slot == 0:
            mine = rotated(mine, cos, sin)
            theirs = rotated(theirs, cos, sin)
        mine_ref[slot] = mine.astype(BF)
        theirs_ref[slot] = theirs.astype(BF)
    part = mul(x_ref[...], w_ref[0])
    scale = scale_ref[...] * (math.log2(math.e) / math.sqrt(HEAD))
    for h in range(2):
        q = rotated(part[:, 128 * h : 128 * h + 128] * scale, cos, sin).astype(BF)
        for dest in range(4):
            q_ref[4 * h + dest] = q


def stage_kernel(*refs):
    keys_ref, values_ref = refs[4:]
    for n, piece in enumerate(refs[:4]):
        keys_ref[256 * n : 256 * n + 256] = piece[0]
        values_ref[:, 256 * n : 256 * n + 256] = piece[1].astype(F32).T.astype(BF)


def attend_kernel(place_ref, q_ref, keys_ref, values_ref, *rest):
    pieces, (out_ref, new_keys, new_values) = rest[:4], rest[4:]
    x, q, k = place_ref[0], place_ref[1], place_ref[2]
    slots = (2 * x + q, 2 * x + 1 - q, 2 * (1 - x) + q, 2 * (1 - x) + 1 - q)
    for slot, piece in zip(slots, pieces):
        spot = pl.ds(pl.multiple_of(slot * 256, 256), 256)
        new_keys[spot, :] = piece[0]
        new_values[:, spot] = piece[1].astype(F32).T.astype(BF)
    sub = lax.broadcasted_iota(jnp.int32, (256, 256), 0)
    lane = lax.broadcasted_iota(jnp.int32, (256, 256), 1)
    row16 = lax.broadcasted_iota(jnp.int32, (16, 256), 0)

    def block_of(i):
        near = i % 4
        return 8 * (i // 4) + jnp.where(q == 0, near, 7 - near)

    def scores_of(i, used):
        scores = [mul_t(keys_ref[...], q_ref[i])]
        if used:
            now = mul_t(new_keys[: 256 * used], q_ref[i])
            block = (k, 7 - k, 8 + k, 15 - k)[used - 1]
            ahead = (block - block_of(i)) * 256
            last = jnp.where(sub + ahead <= lane, now[256 * used - 256 :], -1e30)
            scores += [now[: 256 * used - 256], last] if used > 1 else [last]
        return jnp.concatenate(scores, axis=0)

    def finish(i, top, total, part):
        out_ref[i, :128] = (part / total).astype(BF)
        level = top + jnp.log2(total)
        a = level.astype(BF).astype(F32)
        b = (level - a).astype(BF).astype(F32)
        c = (level - a - b).astype(BF).astype(F32)
        rows = jnp.where(row16 == 0, a, jnp.where(row16 == 1, b, jnp.where(row16 == 2, c, 0.0)))
        out_ref[i, 128:] = rows.astype(BF)

    def two(tiles, used):
        found = []
        for i, n in zip(tiles, used):
            scores = scores_of(i, n)
            found.append((scores, jnp.max(scores, axis=0, keepdims=True)))
        done = []
        for (scores, top), n in zip(found, used):
            expd = jnp.exp2(scores - top)
            total = jnp.sum(expd, axis=0, keepdims=True)
            expd = expd.astype(BF)
            part = mul(values_ref[...], expd[:1024])
            if n:
                part = part + mul(new_values[:, : 256 * n], expd[1024:])
            done.append((top, total, part))
        for i, results in zip(tiles, done):
            finish(i, *results)

    def used_by(i):
        return sum(jnp.where(block <= block_of(i), 1, 0) for block in (k, 7 - k, 8 + k, 15 - k))

    def body(j, carry):
        tiles = (2 * j + q, 2 * j + 1 - q)
        low, high = (used_by(i) for i in tiles)
        for n in range(5):
            for more in (0, 1) if n < 4 else (0,):
                pl.when((low == n) & (high == n + more))(functools.partial(two, tiles, (n, n + more)))
        return carry

    lax.fori_loop(0, 4, body, 0)


def combine_kernel(got_ref, out_ref):
    outs = []
    for h in range(2):
        levels = [
            jnp.sum(got_ref[4 * h + k, 128:].astype(F32), axis=0, keepdims=True) for k in range(4)
        ]
        top = jnp.maximum(jnp.maximum(levels[0], levels[1]), jnp.maximum(levels[2], levels[3]))
        shares = [jnp.exp2(level - top) for level in levels]
        total = shares[0] + shares[1] + shares[2] + shares[3]
        acc = jnp.zeros((128, 256), F32)
        for k in range(4):
            acc = acc + got_ref[4 * h + k, :128].astype(F32) * (shares[k] / total)
        outs.append(acc.T)
    value = jnp.concatenate(outs, axis=1).astype(BF)
    for copy in range(8):
        out_ref[copy] = value


def output_own_kernel(place_ref, own_ref, w_ref, hyena_ref, out_ref):
    core = place_ref[3]
    acc = hyena_ref[...].astype(F32)
    for s in range(8):
        acc = acc + mul(own_ref[s], w_ref[2 * s + core])
    out_ref[...] = acc


def output_kernel(place_ref, other_ref, w_ref, part_ref, out_ref):
    core = 1 - place_ref[3]
    acc = part_ref[...]
    for s in range(8):
        acc = acc + mul(other_ref[s], w_ref[2 * s + core])
    out_ref[...] = acc.astype(BF)


def shape(*dims, dtype=BF):
    return jax.ShapeDtypeStruct(dims, dtype)


def rotation(rows, ha_index):
    freqs = 10000.0 ** (-jnp.arange(64, dtype=F32) / 64)
    places = 16 * rows + ha_index * rows + jnp.arange(rows, dtype=jnp.int32)
    angles = places.astype(F32)[:, None] * freqs[None, :]
    cos, sin = jnp.cos(angles), jnp.sin(angles)
    return jnp.stack([jnp.concatenate([cos, cos], 1), jnp.concatenate([-sin, sin], 1)])


X_FLIP = [(i, i ^ 8) for i in range(16)]
Q_FLIP = [(i, i ^ 7) for i in range(16)]
XQ_FLIP = [(i, i ^ 15) for i in range(16)]


def trade(mine, theirs):
    return (
        mine,
        lax.ppermute(mine, "ha", Q_FLIP),
        lax.ppermute(theirs, "ha", X_FLIP),
        lax.ppermute(theirs, "ha", XQ_FLIP),
    )


WHOLE = pl.BlockSpec()
FAR = pl.BlockSpec(memory_space=pltpu.HBM)


def gather_same_core(copies):
    return lax.all_to_all(copies, GP, 0, 0, axis_index_groups=SAME_CORE)


def local(hyena_proj, dskip, filters, resident, cache_kv, norm_gain, w_qkv, w_out):
    ha_index = lax.axis_index("ha")
    core = lax.axis_index("pb") % 2
    z = ha_index % 8
    query_half = z // 4
    place = jnp.stack([ha_index // 8, query_half, jnp.where(query_half == 0, z, 7 - z), core]).astype(jnp.int32)

    gated_t = pl.pallas_call(
        gate_kernel, out_shape=shape(256, 256), name="gate", compiler_params=params(4)
    )(hyena_proj)
    columns = lax.all_to_all(gated_t.reshape(16, 16, 256), "ha", 0, 0).reshape(256, 256)
    prep, outer, gated = pl.pallas_call(
        prepare_kernel,
        out_shape=(shape(4, 512, 128, dtype=F32), shape(256, 256), shape(256, 256)),
        name="prepare",
        compiler_params=params(16),
    )(filters, resident, hyena_proj)
    conv, tiles = pl.pallas_call(
        conv_kernel,
        out_shape=(shape(256, 256), shape(2, 512, 128, dtype=F32)),
        name="convolve",
        compiler_params=params(24),
    )(columns, prep, jnp.asarray(tables()))
    conv = lax.all_to_all(conv.reshape(16, 16, 256), "ha", 0, 0).reshape(256, 256)
    copies, hyena_out = pl.pallas_call(
        hyena_kernel,

        out_shape=(shape(8, 256, 256), shape(256, 256)),
        name="hyena",
        compiler_params=params(6),
    )(conv, gated, outer, dskip.reshape(1, 256))

    own = gather_same_core(copies)
    mine, theirs = pl.pallas_call(
        pick_kernel,
        in_specs=[SMEM, WHOLE, FAR],
        out_shape=(shape(2, 256, 128), shape(2, 256, 128)),
        name="pick",
        compiler_params=params(4),
    )(place, cache_kv, hyena_out)
    own, old, turn = lax.optimization_barrier((own, trade(mine, theirs), rotation(256, ha_index)))
    other = lax.ppermute(own, "pb", OTHER_CORE)
    block_spectrum, token = pl.pallas_call(
        restore_kernel,
        in_specs=[WHOLE, FAR],
        out_shape=(shape(2, 16, 4096, dtype=F32), shape(8, 128, dtype=F32)),
        name="restore",
        compiler_params=params(8),
    )(tiles, own)
    scaled, scale = pl.pallas_call(
        scale_kernel,
        in_specs=[SMEM] + [WHOLE] * 3 + [FAR],
        out_shape=(shape(256, 4096), shape(256, 128, dtype=F32)),
        name="scale",
        compiler_params=params(8),
    )(place, own, other, norm_gain.reshape(16, 1, 256), token)
    q_msg, mine, theirs = pl.pallas_call(
        qkv_kernel,
        in_specs=[SMEM] + [WHOLE] * 4,
        out_shape=(shape(8, 256, 128), shape(2, 256, 128), shape(2, 256, 128)),
        name="project",
        compiler_params=params(16),
    )(place, scaled, scale, jnp.transpose(w_qkv, (1, 0, 2)), turn)
    new = trade(mine, theirs)
    queries = lax.all_to_all(q_msg, "ha", 0, 0, axis_index_groups=NEAR)
    keys, values = pl.pallas_call(
        stage_kernel, out_shape=(shape(1024, 128), shape(128, 1024)), name="stage", compiler_params=params(8)
    )(*old)
    partial = pl.pallas_call(
        attend_kernel,
        in_specs=[SMEM] + [WHOLE] * 7,
        out_shape=shape(8, 144, 256),
        scratch_shapes=[pltpu.VMEM((1024, 128), BF), pltpu.VMEM((128, 1024), BF)],
        name="attend",
        compiler_params=params(20),
    )(place, queries, keys, values, *new)
    got = lax.all_to_all(partial, "ha", 0, 0, axis_index_groups=NEAR)
    copies_out = pl.pallas_call(
        combine_kernel, out_shape=shape(8, 256, 256), name="combine", compiler_params=params(8)
    )(got)
    own = gather_same_core(copies_out)
    other = lax.ppermute(own, "pb", OTHER_CORE)
    w_blocks = w_out.reshape(16, 256, 256)
    part = pl.pallas_call(
        output_own_kernel,
        in_specs=[SMEM, WHOLE, WHOLE, WHOLE],
        out_shape=shape(256, 256, dtype=F32),
        name="output_own",
        compiler_params=params(8),
    )(place, own, w_blocks, hyena_out)
    mixed = pl.pallas_call(
        output_kernel,
        in_specs=[SMEM] + [WHOLE] * 3,
        out_shape=shape(256, 256),
        name="output",
        compiler_params=params(8),
    )(place, other, w_blocks, part)
    return (mixed, block_spectrum)


def solution(mesh):
    return jax.shard_map(
        local,
        mesh=mesh,
        in_specs=(
            P(None, "ha", ("grp", "pb")),
            P(("grp", "pb")),
            P(None, None, ("grp", "pb", "ha"), None),
            P(None, None, ("grp", "pb", "ha"), None),
            P(None, "ha", ("grp", "pb")),
            P(),
            P(None, None, ("grp", "pb")),
            P(None, ("grp", "pb")),
        ),
        out_specs=(P("ha", ("grp", "pb")), P(None, ("grp", "pb", "ha"), None)),
        check_vma=False,
    )
```

```python
import functools
import math

import jax
import jax.numpy as jnp
import ml_dtypes
import numpy as np
from jax import lax
from jax.experimental import pallas as pl
from jax.experimental.pallas import tpu as pltpu
from jax.sharding import PartitionSpec as P

HEAD = 128
BF = jnp.bfloat16
F32 = jnp.float32
GP = ("grp", "pb")
NEAR = [[8 * x + k for x in range(2) for k in range(4)], [8 * x + 7 - k for x in range(2) for k in range(4)]]
SAME_CORE = [[8 * g + 2 * y + c for g in range(2) for y in range(4)] for c in range(2)]
OTHER_CORE = [(j, j ^ 1) for j in range(8)]
SMEM = pl.BlockSpec(memory_space=pltpu.SMEM)


def params(mib):
    return pltpu.CompilerParams(vmem_limit_bytes=mib * 2**20)


def pair(table):
    high = table.astype(ml_dtypes.bfloat16)
    low = (table - high.astype(np.float64)).astype(ml_dtypes.bfloat16)
    return high, low


@functools.cache
def tables():
    s, k1, t = np.arange(16), np.arange(32), np.arange(256)
    eye = np.eye(16)
    angle = 2 * np.pi / 32 * (np.outer(k1, s) % 32)
    compact = np.stack([np.cos(angle), -np.sin(angle)])
    first = np.einsum("rks,cd->rcksd", compact, eye).reshape(1024, 256)
    angle = 2 * np.pi / 8192 * np.outer(k1, t)
    turn = np.stack([np.cos(angle), np.sin(angle)])
    k2 = (4 * np.arange(32)[None, :] + np.arange(4)[:, None]).reshape(-1)
    angle = 2 * np.pi / 256 * (np.outer(t, k2) % 256)
    cos, sin = np.cos(angle), np.sin(angle)
    second = np.block([[cos, -sin], [sin, cos]])
    compact = np.repeat(compact.reshape(64, 16), 16, axis=1)
    fourth = (first.T / 4096.0).reshape(256, 4, 256).transpose(1, 0, 2).reshape(1024, 256)
    rows = [part for table in (compact, turn.reshape(64, 256), second, fourth) for part in pair(table)]
    return np.concatenate(rows)


def split(values):
    high = values.astype(BF)
    return high, (values - high.astype(F32)).astype(BF)


def mul(a, b):
    return jnp.dot(a, b, preferred_element_type=F32)


def mul_t(a, b):
    return lax.dot_general(a, b, (((1,), (1,)), ((), ())), preferred_element_type=F32)


def gate_kernel(proj_ref, turned_ref):
    gated = (proj_ref[1].astype(F32) * proj_ref[2].astype(F32)).astype(BF)
    turned_ref[...] = gated.astype(F32).T.astype(BF)


def to_tiles(nat):
    out = []
    cube = nat.reshape(16, 32, 128)
    for g in range(4):
        tile = cube[4 * g : 4 * g + 4].reshape(128, 128).T
        for c in range(4):
            out.append(
                jnp.concatenate(
                    [tile[32 * q : 32 * q + 32, 32 * c : 32 * c + 32] for q in range(4)], axis=1
                )
            )
    return jnp.concatenate(out, axis=0)


def from_tiles(tiles):
    out = []
    for g in range(4):
        part = tiles[128 * g : 128 * g + 128]
        swapped = jnp.concatenate(
            [
                jnp.concatenate(
                    [part[32 * c : 32 * c + 32, 32 * q : 32 * q + 32] for c in range(4)], axis=1
                )
                for q in range(4)
            ],
            axis=0,
        )
        out.append(swapped.T.reshape(4, 32, 128))
    return jnp.concatenate(out, axis=0).reshape(16, 4096)


def prepare_kernel(filters_ref, resident_ref, proj_ref, out_ref, outer_ref, gated_ref):
    outer_ref[...] = proj_ref[0]
    gated_ref[...] = (proj_ref[1].astype(F32) * proj_ref[2].astype(F32)).astype(BF)
    lane = lax.broadcasted_iota(jnp.int32, (512, 128), 1)
    row = lax.broadcasted_iota(jnp.int32, (512, 128), 0)
    weight = jnp.where((lane == 0) & (row % 32 == 0), 0.5, 1.0)
    real = jnp.zeros((16, 4096), F32)
    imag = jnp.zeros((16, 4096), F32)
    for m in range(2):
        ar, ai = resident_ref[m, 0], resident_ref[m, 1]
        br, bi = filters_ref[m + 1, 0], filters_ref[m + 1, 1]
        real = real + ar * br - ai * bi
        imag = imag + ar * bi + ai * br
    out_ref[0] = to_tiles(filters_ref[0, 0]) * weight
    out_ref[1] = to_tiles(filters_ref[0, 1]) * weight
    out_ref[2] = to_tiles(real) * weight
    out_ref[3] = to_tiles(imag) * weight


def restore_kernel(tiles_ref, cache_ref, far_ref, after_ref, out_ref, token_ref, pack_ref):
    token_ref[...] = jnp.zeros_like(token_ref)
    pack_ref[:2] = cache_ref[2:]
    pack_ref[2:] = far_ref[2:]
    out_ref[0] = from_tiles(tiles_ref[0])
    out_ref[1] = from_tiles(tiles_ref[1])


def conv_kernel(x_ref, prep_ref, table_ref, conv_ref, spec_ref):
    x = x_ref[...]
    channel = lax.broadcasted_iota(jnp.int32, (2, 16, 32, 256), 1)
    lane = lax.broadcasted_iota(jnp.int32, (2, 16, 32, 256), 3)
    own = lane % 16 == channel
    part = jnp.zeros((1024, 256), F32)
    for n in range(2):
        block = table_ref[64 * n : 64 * n + 64].astype(F32).reshape(2, 1, 32, 256)
        block = jnp.where(own, block, 0.0).reshape(1024, 256).astype(BF)
        part = part + mul(block, x)
    turn = table_ref[128:192].astype(F32) + table_ref[192:256].astype(F32)
    cos, sin = turn[:32], turn[32:]
    second = [table_ref[256 + 512 * n : 768 + 512 * n] for n in range(2)]
    real = part[:512].reshape(16, 32, 256)
    imag = part[512:].reshape(16, 32, 256)
    turned = jnp.concatenate(
        [(real * cos + imag * sin).reshape(512, 256), (imag * cos - real * sin).reshape(512, 256)], axis=1
    )
    high, low = split(turned)
    spec = mul(high, second[0]) + mul(low, second[0]) + mul(high, second[1])
    real, imag = spec[:, :128], spec[:, 128:]
    spec_ref[0] = real
    spec_ref[1] = imag
    z = jnp.concatenate(
        [
            real * prep_ref[0] - imag * prep_ref[1] + prep_ref[2],
            real * prep_ref[1] + imag * prep_ref[0] + prep_ref[3],
        ],
        axis=1,
    )
    high, low = split(z)
    back = mul_t(high, second[0]) + mul_t(low, second[0]) + mul_t(high, second[1])
    real = back[:, :256].reshape(16, 32, 256)
    imag = back[:, 256:].reshape(16, 32, 256)
    turned = jnp.concatenate(
        [(real * cos - imag * sin).reshape(512, 256), (real * sin + imag * cos).reshape(512, 256)], axis=0
    )
    high, low = split(turned)
    fourth = [
        jnp.concatenate([table_ref[1280 + 1024 * n + 256 * j : 1536 + 1024 * n + 256 * j] for j in range(4)], axis=1)
        for n in range(2)
    ]
    conv = mul(fourth[0], high) + mul(fourth[0], low) + mul(fourth[1], high)
    conv_ref[...] = conv.astype(BF)


def hyena_kernel(conv_ref, gated_ref, outer_ref, dskip_ref, out_ref, value_ref):
    conv = conv_ref[...].astype(F32).T
    value = outer_ref[...].astype(F32) * (conv + dskip_ref[...] * gated_ref[...].astype(F32))
    value = value.astype(BF)
    value_ref[...] = value
    for copy in range(8):
        out_ref[copy] = value


def pick_kernel(place_ref, cache_ref, after_ref, out_ref):
    own = place_ref[0]
    for n, head in enumerate((own, 1 - own)):
        out_ref[2 * n : 2 * n + 2] = cache_ref[:, :, pl.ds(pl.multiple_of(head * HEAD, HEAD), HEAD)]


def rotated(values, cos, sin):
    return values * cos + pltpu.roll(values, 64, 1) * sin


def scale_kernel(place_ref, own_ref, other_ref, gain_ref, token_ref, x_ref, scale_ref):
    core = place_ref[3]
    square = jnp.zeros((256, 256), F32)
    for s in range(8):
        for ref, which in ((own_ref, core), (other_ref, 1 - core)):
            x = ref[s].astype(F32)
            square = square + x * x
            place = 2 * s + which
            x_ref[:, pl.ds(pl.multiple_of(place * 256, 256), 256)] = (x * gain_ref[place]).astype(BF)
    scale = lax.rsqrt(jnp.sum(square, axis=1, keepdims=True) / 4096.0 + 1e-05)
    scale_ref[...] = jnp.broadcast_to(scale, (256, 128))


def qkv_kernel(place_ref, x_ref, scale_ref, w_ref, turn_ref, q_ref, mine_ref, theirs_ref):
    first = place_ref[0] == 0
    cos, sin = turn_ref[0], turn_ref[1]
    for slot in range(2):
        part = mul(x_ref[...], w_ref[slot + 1])
        low, high = (part[:, 128 * h : 128 * h + 128] * scale_ref[...] for h in range(2))
        mine = jnp.where(first, low, high)
        theirs = jnp.where(first, high, low)
        if slot == 0:
            mine = rotated(mine, cos, sin)
            theirs = rotated(theirs, cos, sin)
        mine_ref[slot] = mine.astype(BF)
        theirs_ref[slot] = theirs.astype(BF)
    part = mul(x_ref[...], w_ref[0])
    scale = scale_ref[...] * (math.log2(math.e) / math.sqrt(HEAD))
    for h in range(2):
        q = rotated(part[:, 128 * h : 128 * h + 128] * scale, cos, sin).astype(BF)
        for dest in range(4):
            q_ref[4 * h + dest] = q


def stage_kernel(cache_ref, far_ref, across_ref, keys_ref, values_ref):
    pieces = ((cache_ref, 0), (far_ref, 0), (across_ref, 0), (across_ref, 2))
    for n, (ref, at) in enumerate(pieces):
        keys_ref[256 * n : 256 * n + 256] = ref[at]
        values_ref[:, 256 * n : 256 * n + 256] = ref[at + 1].astype(F32).T.astype(BF)


def attend_kernel(place_ref, q_ref, keys_ref, values_ref, *rest):
    pieces, (out_ref, new_keys, new_values) = rest[:4], rest[4:]
    x, q, k = place_ref[0], place_ref[1], place_ref[2]
    slots = (2 * x + q, 2 * x + 1 - q, 2 * (1 - x) + q, 2 * (1 - x) + 1 - q)
    for slot, piece in zip(slots, pieces):
        spot = pl.ds(pl.multiple_of(slot * 256, 256), 256)
        new_keys[spot, :] = piece[0]
        new_values[:, spot] = piece[1].astype(F32).T.astype(BF)
    sub = lax.broadcasted_iota(jnp.int32, (256, 256), 0)
    lane = lax.broadcasted_iota(jnp.int32, (256, 256), 1)
    row16 = lax.broadcasted_iota(jnp.int32, (16, 256), 0)

    def block_of(i):
        near = i % 4
        return 8 * (i // 4) + jnp.where(q == 0, near, 7 - near)

    def scores_of(i, used):
        scores = [mul_t(keys_ref[...], q_ref[i])]
        if used:
            now = mul_t(new_keys[: 256 * used], q_ref[i])
            block = (k, 7 - k, 8 + k, 15 - k)[used - 1]
            ahead = (block - block_of(i)) * 256
            last = jnp.where(sub + ahead <= lane, now[256 * used - 256 :], -1e30)
            scores += [now[: 256 * used - 256], last] if used > 1 else [last]
        return jnp.concatenate(scores, axis=0)

    def finish(i, top, total, part):
        out_ref[i, :128] = (part / total).astype(BF)
        level = top + jnp.log2(total)
        a = level.astype(BF).astype(F32)
        b = (level - a).astype(BF).astype(F32)
        c = (level - a - b).astype(BF).astype(F32)
        rows = jnp.where(row16 == 0, a, jnp.where(row16 == 1, b, jnp.where(row16 == 2, c, 0.0)))
        out_ref[i, 128:] = rows.astype(BF)

    def two(tiles, used):
        found = []
        for i, n in zip(tiles, used):
            scores = scores_of(i, n)
            found.append((scores, jnp.max(scores, axis=0, keepdims=True)))
        done = []
        for (scores, top), n in zip(found, used):
            expd = jnp.exp2(scores - top)
            total = jnp.sum(expd, axis=0, keepdims=True)
            expd = expd.astype(BF)
            part = mul(values_ref[...], expd[:1024])
            if n:
                part = part + mul(new_values[:, : 256 * n], expd[1024:])
            done.append((top, total, part))
        for i, results in zip(tiles, done):
            finish(i, *results)

    def used_by(i):
        return sum(jnp.where(block <= block_of(i), 1, 0) for block in (k, 7 - k, 8 + k, 15 - k))

    def body(j, carry):
        tiles = (2 * j + q, 2 * j + 1 - q)
        low, high = (used_by(i) for i in tiles)
        for n in range(5):
            for more in (0, 1) if n < 4 else (0,):
                pl.when((low == n) & (high == n + more))(functools.partial(two, tiles, (n, n + more)))
        return carry

    lax.fori_loop(0, 4, body, 0)


def combine_kernel(got_ref, out_ref):
    outs = []
    for h in range(2):
        levels = [
            jnp.sum(got_ref[4 * h + k, 128:].astype(F32), axis=0, keepdims=True) for k in range(4)
        ]
        top = jnp.maximum(jnp.maximum(levels[0], levels[1]), jnp.maximum(levels[2], levels[3]))
        shares = [jnp.exp2(level - top) for level in levels]
        total = shares[0] + shares[1] + shares[2] + shares[3]
        acc = jnp.zeros((128, 256), F32)
        for k in range(4):
            acc = acc + got_ref[4 * h + k, :128].astype(F32) * (shares[k] / total)
        outs.append(acc.T)
    value = jnp.concatenate(outs, axis=1).astype(BF)
    for copy in range(8):
        out_ref[copy] = value


def output_own_kernel(place_ref, own_ref, w_ref, hyena_ref, out_ref):
    core = place_ref[3]
    acc = hyena_ref[...].astype(F32)
    for s in range(8):
        acc = acc + mul(own_ref[s], w_ref[2 * s + core])
    out_ref[...] = acc


def output_kernel(place_ref, other_ref, w_ref, part_ref, out_ref):
    core = 1 - place_ref[3]
    acc = part_ref[...]
    for s in range(8):
        acc = acc + mul(other_ref[s], w_ref[2 * s + core])
    out_ref[...] = acc.astype(BF)


def shape(*dims, dtype=BF):
    return jax.ShapeDtypeStruct(dims, dtype)


def rotation(rows, ha_index):
    freqs = 10000.0 ** (-jnp.arange(64, dtype=F32) / 64)
    places = 16 * rows + ha_index * rows + jnp.arange(rows, dtype=jnp.int32)
    angles = places.astype(F32)[:, None] * freqs[None, :]
    cos, sin = jnp.cos(angles), jnp.sin(angles)
    return jnp.stack([jnp.concatenate([cos, cos], 1), jnp.concatenate([-sin, sin], 1)])


X_FLIP = [(i, i ^ 8) for i in range(16)]
Q_FLIP = [(i, i ^ 7) for i in range(16)]
XQ_FLIP = [(i, i ^ 15) for i in range(16)]


def trade(mine, theirs):
    return (
        mine,
        lax.ppermute(mine, "ha", Q_FLIP),
        lax.ppermute(theirs, "ha", X_FLIP),
        lax.ppermute(theirs, "ha", XQ_FLIP),
    )


WHOLE = pl.BlockSpec()
FAR = pl.BlockSpec(memory_space=pltpu.HBM)


def gather_same_core(copies):
    return lax.all_to_all(copies, GP, 0, 0, axis_index_groups=SAME_CORE)


def local(hyena_proj, dskip, filters, resident, cache_kv, norm_gain, w_qkv, w_out):
    ha_index = lax.axis_index("ha")
    core = lax.axis_index("pb") % 2
    z = ha_index % 8
    query_half = z // 4
    place = jnp.stack([ha_index // 8, query_half, jnp.where(query_half == 0, z, 7 - z), core]).astype(jnp.int32)

    gated_t = pl.pallas_call(
        gate_kernel, out_shape=shape(256, 256), name="gate", compiler_params=params(4)
    )(hyena_proj)
    columns = lax.all_to_all(gated_t.reshape(16, 16, 256), "ha", 0, 0).reshape(256, 256)
    prep, outer, gated = pl.pallas_call(
        prepare_kernel,
        out_shape=(shape(4, 512, 128, dtype=F32), shape(256, 256), shape(256, 256)),
        name="prepare",
        compiler_params=params(16),
    )(filters, resident, hyena_proj)
    conv, tiles = pl.pallas_call(
        conv_kernel,
        out_shape=(shape(256, 256), shape(2, 512, 128, dtype=F32)),
        name="convolve",
        compiler_params=params(24),
    )(columns, prep, jnp.asarray(tables()))
    conv = lax.all_to_all(conv.reshape(16, 16, 256), "ha", 0, 0).reshape(256, 256)
    copies, hyena_out = pl.pallas_call(
        hyena_kernel,

        out_shape=(shape(8, 256, 256), shape(256, 256)),
        name="hyena",
        compiler_params=params(6),
    )(conv, gated, outer, dskip.reshape(1, 256))

    own = gather_same_core(copies)
    cache = pl.pallas_call(
        pick_kernel,
        in_specs=[SMEM, WHOLE, FAR],
        out_shape=shape(4, 256, 128),
        name="pick",
        compiler_params=params(4),
    )(place, cache_kv, hyena_out)
    own, far, turn = lax.optimization_barrier(
        (own, lax.ppermute(cache, "ha", Q_FLIP), rotation(256, ha_index))
    )
    other = lax.ppermute(own, "pb", OTHER_CORE)
    block_spectrum, token, pack = pl.pallas_call(
        restore_kernel,
        in_specs=[WHOLE] * 3 + [FAR],
        out_shape=(shape(2, 16, 4096, dtype=F32), shape(8, 128, dtype=F32), shape(4, 256, 128)),
        name="restore",
        compiler_params=params(8),
    )(tiles, cache, far, own)
    across = lax.ppermute(pack, "ha", X_FLIP)
    scaled, scale = pl.pallas_call(
        scale_kernel,
        in_specs=[SMEM] + [WHOLE] * 3 + [FAR],
        out_shape=(shape(256, 4096), shape(256, 128, dtype=F32)),
        name="scale",
        compiler_params=params(8),
    )(place, own, other, norm_gain.reshape(16, 1, 256), token)
    q_msg, mine, theirs = pl.pallas_call(
        qkv_kernel,
        in_specs=[SMEM] + [WHOLE] * 4,
        out_shape=(shape(8, 256, 128), shape(2, 256, 128), shape(2, 256, 128)),
        name="project",
        compiler_params=params(16),
    )(place, scaled, scale, jnp.transpose(w_qkv, (1, 0, 2)), turn)
    new = trade(mine, theirs)
    queries = lax.all_to_all(q_msg, "ha", 0, 0, axis_index_groups=NEAR)
    keys, values = pl.pallas_call(
        stage_kernel, out_shape=(shape(1024, 128), shape(128, 1024)), name="stage", compiler_params=params(8)
    )(cache, far, across)
    partial = pl.pallas_call(
        attend_kernel,
        in_specs=[SMEM] + [WHOLE] * 7,
        out_shape=shape(8, 144, 256),
        scratch_shapes=[pltpu.VMEM((1024, 128), BF), pltpu.VMEM((128, 1024), BF)],
        name="attend",
        compiler_params=params(20),
    )(place, queries, keys, values, *new)
    got = lax.all_to_all(partial, "ha", 0, 0, axis_index_groups=NEAR)
    copies_out = pl.pallas_call(
        combine_kernel, out_shape=shape(8, 256, 256), name="combine", compiler_params=params(8)
    )(got)
    own = gather_same_core(copies_out)
    other = lax.ppermute(own, "pb", OTHER_CORE)
    w_blocks = w_out.reshape(16, 256, 256)
    part = pl.pallas_call(
        output_own_kernel,
        in_specs=[SMEM, WHOLE, WHOLE, WHOLE],
        out_shape=shape(256, 256, dtype=F32),
        name="output_own",
        compiler_params=params(8),
    )(place, own, w_blocks, hyena_out)
    mixed = pl.pallas_call(
        output_kernel,
        in_specs=[SMEM] + [WHOLE] * 3,
        out_shape=shape(256, 256),
        name="output",
        compiler_params=params(8),
    )(place, other, w_blocks, part)
    return (mixed, block_spectrum)


def solution(mesh):
    return jax.shard_map(
        local,
        mesh=mesh,
        in_specs=(
            P(None, "ha", ("grp", "pb")),
            P(("grp", "pb")),
            P(None, None, ("grp", "pb", "ha"), None),
            P(None, None, ("grp", "pb", "ha"), None),
            P(None, "ha", ("grp", "pb")),
            P(),
            P(None, None, ("grp", "pb")),
            P(None, ("grp", "pb")),
        ),
        out_specs=(P("ha", ("grp", "pb")), P(None, ("grp", "pb", "ha"), None)),
        check_vma=False,
    )
```

```python
import functools
import math

import jax
import jax.numpy as jnp
import ml_dtypes
import numpy as np
from jax import lax
from jax.experimental import pallas as pl
from jax.experimental.pallas import tpu as pltpu
from jax.sharding import PartitionSpec as P

HEAD = 128
BF = jnp.bfloat16
F32 = jnp.float32
GP = ("grp", "pb")
NEAR = [[8 * x + k for x in range(2) for k in range(4)], [8 * x + 7 - k for x in range(2) for k in range(4)]]
SAME_CORE = [[8 * g + 2 * y + c for g in range(2) for y in range(4)] for c in range(2)]
OTHER_CORE = [(j, j ^ 1) for j in range(8)]
SMEM = pl.BlockSpec(memory_space=pltpu.SMEM)


def params(mib):
    return pltpu.CompilerParams(vmem_limit_bytes=mib * 2**20)


def pair(table):
    high = table.astype(ml_dtypes.bfloat16)
    low = (table - high.astype(np.float64)).astype(ml_dtypes.bfloat16)
    return high, low


@functools.cache
def tables():
    s, k1, t = np.arange(16), np.arange(32), np.arange(256)
    eye = np.eye(16)
    angle = 2 * np.pi / 32 * (np.outer(k1, s) % 32)
    compact = np.stack([np.cos(angle), -np.sin(angle)])
    first = np.einsum("rks,cd->rcksd", compact, eye).reshape(1024, 256)
    angle = 2 * np.pi / 8192 * np.outer(k1, t)
    turn = np.stack([np.cos(angle), np.sin(angle)])
    k2 = (4 * np.arange(32)[None, :] + np.arange(4)[:, None]).reshape(-1)
    angle = 2 * np.pi / 256 * (np.outer(t, k2) % 256)
    cos, sin = np.cos(angle), np.sin(angle)
    second = np.block([[cos, -sin], [sin, cos]])
    compact = np.repeat(compact.reshape(64, 16), 16, axis=1)
    fourth = (first.T / 4096.0).reshape(256, 4, 256).transpose(1, 0, 2).reshape(1024, 256)
    rows = [part for table in (compact, turn.reshape(64, 256), second, fourth) for part in pair(table)]
    return np.concatenate(rows)


def split(values):
    high = values.astype(BF)
    return high, (values - high.astype(F32)).astype(BF)


def mul(a, b):
    return jnp.dot(a, b, preferred_element_type=F32)


def mul_t(a, b):
    return lax.dot_general(a, b, (((1,), (1,)), ((), ())), preferred_element_type=F32)


def gate_kernel(proj_ref, turned_ref):
    gated = (proj_ref[1].astype(F32) * proj_ref[2].astype(F32)).astype(BF)
    turned_ref[...] = gated.astype(F32).T.astype(BF)


def to_tiles(nat):
    out = []
    cube = nat.reshape(16, 32, 128)
    for g in range(4):
        tile = cube[4 * g : 4 * g + 4].reshape(128, 128).T
        for c in range(4):
            out.append(
                jnp.concatenate(
                    [tile[32 * q : 32 * q + 32, 32 * c : 32 * c + 32] for q in range(4)], axis=1
                )
            )
    return jnp.concatenate(out, axis=0)


def from_tiles(tiles):
    out = []
    for g in range(4):
        part = tiles[128 * g : 128 * g + 128]
        swapped = jnp.concatenate(
            [
                jnp.concatenate(
                    [part[32 * c : 32 * c + 32, 32 * q : 32 * q + 32] for c in range(4)], axis=1
                )
                for q in range(4)
            ],
            axis=0,
        )
        out.append(swapped.T.reshape(4, 32, 128))
    return jnp.concatenate(out, axis=0).reshape(16, 4096)


def prepare_kernel(filters_ref, resident_ref, proj_ref, out_ref, outer_ref, gated_ref):
    outer_ref[...] = proj_ref[0]
    gated_ref[...] = (proj_ref[1].astype(F32) * proj_ref[2].astype(F32)).astype(BF)
    lane = lax.broadcasted_iota(jnp.int32, (512, 128), 1)
    row = lax.broadcasted_iota(jnp.int32, (512, 128), 0)
    weight = jnp.where((lane == 0) & (row % 32 == 0), 0.5, 1.0)
    real = jnp.zeros((16, 4096), F32)
    imag = jnp.zeros((16, 4096), F32)
    for m in range(2):
        ar, ai = resident_ref[m, 0], resident_ref[m, 1]
        br, bi = filters_ref[m + 1, 0], filters_ref[m + 1, 1]
        real = real + ar * br - ai * bi
        imag = imag + ar * bi + ai * br
    out_ref[0] = to_tiles(filters_ref[0, 0]) * weight
    out_ref[1] = to_tiles(filters_ref[0, 1]) * weight
    out_ref[2] = to_tiles(real) * weight
    out_ref[3] = to_tiles(imag) * weight


def restore_kernel(tiles_ref, cache_ref, far_ref, after_ref, out_ref, token_ref, pack_ref):
    token_ref[...] = jnp.zeros_like(token_ref)
    pack_ref[:2] = cache_ref[2:]
    pack_ref[2:] = far_ref[2:]
    out_ref[0] = from_tiles(tiles_ref[0])
    out_ref[1] = from_tiles(tiles_ref[1])


def conv_kernel(x_ref, prep_ref, table_ref, conv_ref, spec_ref):
    x = x_ref[...]
    channel = lax.broadcasted_iota(jnp.int32, (2, 16, 32, 256), 1)
    lane = lax.broadcasted_iota(jnp.int32, (2, 16, 32, 256), 3)
    own = lane % 16 == channel
    part = jnp.zeros((1024, 256), F32)
    for n in range(2):
        block = table_ref[64 * n : 64 * n + 64].astype(F32).reshape(2, 1, 32, 256)
        block = jnp.where(own, block, 0.0).reshape(1024, 256).astype(BF)
        part = part + mul(block, x)
    turn = table_ref[128:192].astype(F32) + table_ref[192:256].astype(F32)
    cos, sin = turn[:32], turn[32:]
    second = [table_ref[256 + 512 * n : 768 + 512 * n] for n in range(2)]
    real = part[:512].reshape(16, 32, 256)
    imag = part[512:].reshape(16, 32, 256)
    turned = jnp.concatenate(
        [(real * cos + imag * sin).reshape(512, 256), (imag * cos - real * sin).reshape(512, 256)], axis=1
    )
    high, low = split(turned)
    spec = mul(high, second[0]) + mul(low, second[0]) + mul(high, second[1])
    real, imag = spec[:, :128], spec[:, 128:]
    spec_ref[0] = real
    spec_ref[1] = imag
    z = jnp.concatenate(
        [
            real * prep_ref[0] - imag * prep_ref[1] + prep_ref[2],
            real * prep_ref[1] + imag * prep_ref[0] + prep_ref[3],
        ],
        axis=1,
    )
    high, low = split(z)
    back = mul_t(high, second[0]) + mul_t(low, second[0]) + mul_t(high, second[1])
    real = back[:, :256].reshape(16, 32, 256)
    imag = back[:, 256:].reshape(16, 32, 256)
    turned = jnp.concatenate(
        [(real * cos - imag * sin).reshape(512, 256), (real * sin + imag * cos).reshape(512, 256)], axis=0
    )
    high, low = split(turned)
    fourth = [
        jnp.concatenate([table_ref[1280 + 1024 * n + 256 * j : 1536 + 1024 * n + 256 * j] for j in range(4)], axis=1)
        for n in range(2)
    ]
    conv = mul(fourth[0], high) + mul(fourth[0], low) + mul(fourth[1], high)
    conv_ref[...] = conv.astype(BF)


def hyena_kernel(conv_ref, gated_ref, outer_ref, dskip_ref, out_ref, value_ref):
    conv = conv_ref[...].astype(F32).T
    value = outer_ref[...].astype(F32) * (conv + dskip_ref[...] * gated_ref[...].astype(F32))
    value = value.astype(BF)
    value_ref[...] = value
    for copy in range(8):
        out_ref[copy] = value


def pick_kernel(place_ref, cache_ref, after_ref, out_ref):
    own = place_ref[0]
    for n, head in enumerate((own, 1 - own)):
        out_ref[2 * n : 2 * n + 2] = cache_ref[:, :, pl.ds(pl.multiple_of(head * HEAD, HEAD), HEAD)]


def rotated(values, cos, sin):
    return values * cos + pltpu.roll(values, 64, 1) * sin


def scale_kernel(place_ref, own_ref, other_ref, gain_ref, token_ref, x_ref, scale_ref):
    core = place_ref[3]
    square = jnp.zeros((256, 256), F32)
    for s in range(8):
        for ref, which in ((own_ref, core), (other_ref, 1 - core)):
            x = ref[s].astype(F32)
            square = square + x * x
            place = 2 * s + which
            x_ref[:, pl.ds(pl.multiple_of(place * 256, 256), 256)] = (x * gain_ref[place]).astype(BF)
    scale = lax.rsqrt(jnp.sum(square, axis=1, keepdims=True) / 4096.0 + 1e-05)
    scale_ref[...] = jnp.broadcast_to(scale, (256, 128))


def keys_kernel(place_ref, x_ref, scale_ref, wk_ref, wv_ref, turn_ref, mine_ref, theirs_ref):
    first = place_ref[0] == 0
    for slot, w_ref in enumerate((wk_ref, wv_ref)):
        part = mul(x_ref[...], w_ref[...])
        low, high = (part[:, 128 * h : 128 * h + 128] * scale_ref[...] for h in range(2))
        mine = jnp.where(first, low, high)
        theirs = jnp.where(first, high, low)
        if slot == 0:
            mine = rotated(mine, turn_ref[0], turn_ref[1])
            theirs = rotated(theirs, turn_ref[0], turn_ref[1])
        mine_ref[slot] = mine.astype(BF)
        theirs_ref[slot] = theirs.astype(BF)


def queries_kernel(x_ref, scale_ref, w_ref, turn_ref, after_ref, q_ref):
    part = mul(x_ref[...], w_ref[...])
    scale = scale_ref[...] * (math.log2(math.e) / math.sqrt(HEAD))
    for h in range(2):
        q = rotated(part[:, 128 * h : 128 * h + 128] * scale, turn_ref[0], turn_ref[1]).astype(BF)
        for dest in range(4):
            q_ref[4 * h + dest] = q


def stage_kernel(cache_ref, far_ref, across_ref, keys_ref, values_ref):
    pieces = ((cache_ref, 0), (far_ref, 0), (across_ref, 0), (across_ref, 2))
    for n, (ref, at) in enumerate(pieces):
        keys_ref[256 * n : 256 * n + 256] = ref[at]
        values_ref[:, 256 * n : 256 * n + 256] = ref[at + 1].astype(F32).T.astype(BF)


def attend_kernel(place_ref, q_ref, keys_ref, values_ref, *rest):
    pieces, (out_ref, new_keys, new_values) = rest[:4], rest[4:]
    x, q, k = place_ref[0], place_ref[1], place_ref[2]
    slots = (2 * x + q, 2 * x + 1 - q, 2 * (1 - x) + q, 2 * (1 - x) + 1 - q)
    for slot, piece in zip(slots, pieces):
        spot = pl.ds(pl.multiple_of(slot * 256, 256), 256)
        new_keys[spot, :] = piece[0]
        new_values[:, spot] = piece[1].astype(F32).T.astype(BF)
    sub = lax.broadcasted_iota(jnp.int32, (256, 256), 0)
    lane = lax.broadcasted_iota(jnp.int32, (256, 256), 1)
    row16 = lax.broadcasted_iota(jnp.int32, (16, 256), 0)

    def block_of(i):
        near = i % 4
        return 8 * (i // 4) + jnp.where(q == 0, near, 7 - near)

    def scores_of(i, used):
        scores = [mul_t(keys_ref[...], q_ref[i])]
        if used:
            now = mul_t(new_keys[: 256 * used], q_ref[i])
            block = (k, 7 - k, 8 + k, 15 - k)[used - 1]
            ahead = (block - block_of(i)) * 256
            last = jnp.where(sub + ahead <= lane, now[256 * used - 256 :], -1e30)
            scores += [now[: 256 * used - 256], last] if used > 1 else [last]
        return jnp.concatenate(scores, axis=0)

    def finish(i, top, total, part):
        out_ref[i, :128] = (part / total).astype(BF)
        level = top + jnp.log2(total)
        a = level.astype(BF).astype(F32)
        b = (level - a).astype(BF).astype(F32)
        c = (level - a - b).astype(BF).astype(F32)
        rows = jnp.where(row16 == 0, a, jnp.where(row16 == 1, b, jnp.where(row16 == 2, c, 0.0)))
        out_ref[i, 128:] = rows.astype(BF)

    def two(tiles, used):
        found = []
        for i, n in zip(tiles, used):
            scores = scores_of(i, n)
            found.append((scores, jnp.max(scores, axis=0, keepdims=True)))
        done = []
        for (scores, top), n in zip(found, used):
            expd = jnp.exp2(scores - top)
            total = jnp.sum(expd, axis=0, keepdims=True)
            expd = expd.astype(BF)
            part = mul(values_ref[...], expd[:1024])
            if n:
                part = part + mul(new_values[:, : 256 * n], expd[1024:])
            done.append((top, total, part))
        for i, results in zip(tiles, done):
            finish(i, *results)

    def used_by(i):
        return sum(jnp.where(block <= block_of(i), 1, 0) for block in (k, 7 - k, 8 + k, 15 - k))

    def body(j, carry):
        tiles = (2 * j + q, 2 * j + 1 - q)
        low, high = (used_by(i) for i in tiles)
        for n in range(5):
            for more in (0, 1) if n < 4 else (0,):
                pl.when((low == n) & (high == n + more))(functools.partial(two, tiles, (n, n + more)))
        return carry

    lax.fori_loop(0, 4, body, 0)


def combine_kernel(got_ref, out_ref):
    outs = []
    for h in range(2):
        levels = [
            jnp.sum(got_ref[4 * h + k, 128:].astype(F32), axis=0, keepdims=True) for k in range(4)
        ]
        top = jnp.maximum(jnp.maximum(levels[0], levels[1]), jnp.maximum(levels[2], levels[3]))
        shares = [jnp.exp2(level - top) for level in levels]
        total = shares[0] + shares[1] + shares[2] + shares[3]
        acc = jnp.zeros((128, 256), F32)
        for k in range(4):
            acc = acc + got_ref[4 * h + k, :128].astype(F32) * (shares[k] / total)
        outs.append(acc.T)
    value = jnp.concatenate(outs, axis=1).astype(BF)
    for copy in range(8):
        out_ref[copy] = value


def output_own_kernel(place_ref, own_ref, w_ref, hyena_ref, out_ref):
    core = place_ref[3]
    acc = hyena_ref[...].astype(F32)
    for s in range(8):
        acc = acc + mul(own_ref[s], w_ref[2 * s + core])
    out_ref[...] = acc


def output_kernel(place_ref, other_ref, w_ref, part_ref, out_ref):
    core = 1 - place_ref[3]
    acc = part_ref[...]
    for s in range(8):
        acc = acc + mul(other_ref[s], w_ref[2 * s + core])
    out_ref[...] = acc.astype(BF)


def shape(*dims, dtype=BF):
    return jax.ShapeDtypeStruct(dims, dtype)


def rotation(rows, ha_index):
    freqs = 10000.0 ** (-jnp.arange(64, dtype=F32) / 64)
    places = 16 * rows + ha_index * rows + jnp.arange(rows, dtype=jnp.int32)
    angles = places.astype(F32)[:, None] * freqs[None, :]
    cos, sin = jnp.cos(angles), jnp.sin(angles)
    return jnp.stack([jnp.concatenate([cos, cos], 1), jnp.concatenate([-sin, sin], 1)])


X_FLIP = [(i, i ^ 8) for i in range(16)]
Q_FLIP = [(i, i ^ 7) for i in range(16)]
XQ_FLIP = [(i, i ^ 15) for i in range(16)]


def trade(mine, theirs):
    return (
        mine,
        lax.ppermute(mine, "ha", Q_FLIP),
        lax.ppermute(theirs, "ha", X_FLIP),
        lax.ppermute(theirs, "ha", XQ_FLIP),
    )


WHOLE = pl.BlockSpec()
FAR = pl.BlockSpec(memory_space=pltpu.HBM)


def gather_same_core(copies):
    return lax.all_to_all(copies, GP, 0, 0, axis_index_groups=SAME_CORE)


def local(hyena_proj, dskip, filters, resident, cache_kv, norm_gain, w_qkv, w_out):
    ha_index = lax.axis_index("ha")
    core = lax.axis_index("pb") % 2
    z = ha_index % 8
    query_half = z // 4
    place = jnp.stack([ha_index // 8, query_half, jnp.where(query_half == 0, z, 7 - z), core]).astype(jnp.int32)

    gated_t = pl.pallas_call(
        gate_kernel, out_shape=shape(256, 256), name="gate", compiler_params=params(4)
    )(hyena_proj)
    columns = lax.all_to_all(gated_t.reshape(16, 16, 256), "ha", 0, 0).reshape(256, 256)
    prep, outer, gated = pl.pallas_call(
        prepare_kernel,
        out_shape=(shape(4, 512, 128, dtype=F32), shape(256, 256), shape(256, 256)),
        name="prepare",
        compiler_params=params(16),
    )(filters, resident, hyena_proj)
    conv, tiles = pl.pallas_call(
        conv_kernel,
        out_shape=(shape(256, 256), shape(2, 512, 128, dtype=F32)),
        name="convolve",
        compiler_params=params(24),
    )(columns, prep, jnp.asarray(tables()))
    conv = lax.all_to_all(conv.reshape(16, 16, 256), "ha", 0, 0).reshape(256, 256)
    copies, hyena_out = pl.pallas_call(
        hyena_kernel,

        out_shape=(shape(8, 256, 256), shape(256, 256)),
        name="hyena",
        compiler_params=params(6),
    )(conv, gated, outer, dskip.reshape(1, 256))

    own = gather_same_core(copies)
    cache = pl.pallas_call(
        pick_kernel,
        in_specs=[SMEM, WHOLE, FAR],
        out_shape=shape(4, 256, 128),
        name="pick",
        compiler_params=params(4),
    )(place, cache_kv, hyena_out)
    own, far, turn = lax.optimization_barrier(
        (own, lax.ppermute(cache, "ha", Q_FLIP), rotation(256, ha_index))
    )
    other = lax.ppermute(own, "pb", OTHER_CORE)
    block_spectrum, token, pack = pl.pallas_call(
        restore_kernel,
        in_specs=[WHOLE] * 3 + [FAR],
        out_shape=(shape(2, 16, 4096, dtype=F32), shape(8, 128, dtype=F32), shape(4, 256, 128)),
        name="restore",
        compiler_params=params(8),
    )(tiles, cache, far, own)
    across = lax.ppermute(pack, "ha", X_FLIP)
    scaled, scale = pl.pallas_call(
        scale_kernel,
        in_specs=[SMEM] + [WHOLE] * 3 + [FAR],
        out_shape=(shape(256, 4096), shape(256, 128, dtype=F32)),
        name="scale",
        compiler_params=params(8),
    )(place, own, other, norm_gain.reshape(16, 1, 256), token)
    w_parts = jnp.transpose(w_qkv, (1, 0, 2))
    mine, theirs = pl.pallas_call(
        keys_kernel,
        in_specs=[SMEM] + [WHOLE] * 5,
        out_shape=(shape(2, 256, 128), shape(2, 256, 128)),
        name="project_keys",
        compiler_params=params(12),
    )(place, scaled, scale, w_parts[1], w_parts[2], turn)
    new = trade(mine, theirs)
    q_msg = pl.pallas_call(
        queries_kernel,
        in_specs=[WHOLE] * 4 + [FAR],
        out_shape=shape(8, 256, 128),
        name="project_queries",
        compiler_params=params(12),
    )(scaled, scale, w_parts[0], turn, mine)
    queries = lax.all_to_all(q_msg, "ha", 0, 0, axis_index_groups=NEAR)
    keys, values = pl.pallas_call(
        stage_kernel, out_shape=(shape(1024, 128), shape(128, 1024)), name="stage", compiler_params=params(8)
    )(cache, far, across)
    partial = pl.pallas_call(
        attend_kernel,
        in_specs=[SMEM] + [WHOLE] * 7,
        out_shape=shape(8, 144, 256),
        scratch_shapes=[pltpu.VMEM((1024, 128), BF), pltpu.VMEM((128, 1024), BF)],
        name="attend",
        compiler_params=params(20),
    )(place, queries, keys, values, *new)
    got = lax.all_to_all(partial, "ha", 0, 0, axis_index_groups=NEAR)
    copies_out = pl.pallas_call(
        combine_kernel, out_shape=shape(8, 256, 256), name="combine", compiler_params=params(8)
    )(got)
    own = gather_same_core(copies_out)
    other = lax.ppermute(own, "pb", OTHER_CORE)
    w_blocks = w_out.reshape(16, 256, 256)
    part = pl.pallas_call(
        output_own_kernel,
        in_specs=[SMEM, WHOLE, WHOLE, WHOLE],
        out_shape=shape(256, 256, dtype=F32),
        name="output_own",
        compiler_params=params(8),
    )(place, own, w_blocks, hyena_out)
    mixed = pl.pallas_call(
        output_kernel,
        in_specs=[SMEM] + [WHOLE] * 3,
        out_shape=shape(256, 256),
        name="output",
        compiler_params=params(8),
    )(place, other, w_blocks, part)
    return (mixed, block_spectrum)


def solution(mesh):
    return jax.shard_map(
        local,
        mesh=mesh,
        in_specs=(
            P(None, "ha", ("grp", "pb")),
            P(("grp", "pb")),
            P(None, None, ("grp", "pb", "ha"), None),
            P(None, None, ("grp", "pb", "ha"), None),
            P(None, "ha", ("grp", "pb")),
            P(),
            P(None, None, ("grp", "pb")),
            P(None, ("grp", "pb")),
        ),
        out_specs=(P("ha", ("grp", "pb")), P(None, ("grp", "pb", "ha"), None)),
        check_vma=False,
    )
```
